32 devices in a mesh: dp: 8 (over z, x), mp: 4 (over y, core).
Axes of the slice: x: 2, y: 2, z: 4, core: 2. Of those that a mesh axis runs over, the one named last changes fastest.
Arguments:
- x_lo: bfloat16 [96, 196, 768], P('dp', 'mp'), may hold values from -45 to 45
- x_hi: bfloat16 [16, 576, 768], P('dp', 'mp'), may hold values from -45 to 45
- cot_lo: bfloat16 [96, 196, 768], P('dp', 'mp'), may hold values from -6 to 6
- cot_hi: bfloat16 [16, 576, 768], P('dp', 'mp'), may hold values from -6 to 6
- counts: int32 [8, 2], P('dp'), may hold values from 1 to 12, as said below
- ln1_gain: bfloat16 [768], replicated, may hold values from 0.099609375 to 1.8984375
- ln1_bias: bfloat16 [768], replicated, may hold values from -3 to 3
- w_tok1_lo: bfloat16 [196, 384], P(None, 'mp'), may hold values from -0.4375 to 0.4375
- b_tok1_lo: bfloat16 [384], P('mp'), may hold values from -3 to 3
- w_tok2_lo: bfloat16 [384, 196], P('mp'), may hold values from -0.3125 to 0.3125
- b_tok2_lo: bfloat16 [196], P('mp'), may hold values from -3 to 3
- w_tok1_hi: bfloat16 [576, 384], P(None, 'mp'), may hold values from -0.25 to 0.25
- b_tok1_hi: bfloat16 [384], P('mp'), may hold values from -3 to 3
- w_tok2_hi: bfloat16 [384, 576], P('mp'), may hold values from -0.3125 to 0.3125
- b_tok2_hi: bfloat16 [576], P('mp'), may hold values from -3 to 3
- ln2_gain: bfloat16 [768], replicated, may hold values from 0.099609375 to 1.8984375
- ln2_bias: bfloat16 [768], replicated, may hold values from -3 to 3
- w_chan_in: bfloat16 [768, 3072], replicated, may hold values from -0.21875 to 0.21875
- b_chan_in: bfloat16 [3072], replicated, may hold values from -3 to 3
- w_chan_out: bfloat16 [3072, 768], replicated, may hold values from -0.109375 to 0.109375
- b_chan_out: bfloat16 [768], replicated, may hold values from -3 to 3
Outputs:
- out_lo: bfloat16 [96, 196, 768], P('dp', 'mp')
- out_hi: bfloat16 [16, 576, 768], P('dp', 'mp')
- grad_lo: float32 [96, 196, 768], P('dp', 'mp')
- grad_hi: float32 [16, 576, 768], P('dp', 'mp')
- g_ln1_gain: float32 [768], replicated
- g_ln1_bias: float32 [768], replicated
- g_w_tok1_lo: float32 [196, 384], P(None, 'mp')
- g_b_tok1_lo: float32 [384], P('mp')
- g_w_tok2_lo: float32 [384, 196], P('mp')
- g_b_tok2_lo: float32 [196], P('mp')
- g_w_tok1_hi: float32 [576, 384], P(None, 'mp')
- g_b_tok1_hi: float32 [384], P('mp')
- g_w_tok2_hi: float32 [384, 576], P('mp')
- g_b_tok2_hi: float32 [576], P('mp')
- g_ln2_gain: float32 [768], replicated
- g_ln2_bias: float32 [768], replicated
- g_w_chan_in: float32 [768, 3072], replicated
- g_b_chan_in: float32 [3072], replicated
- g_w_chan_out: float32 [3072, 768], replicated
- g_b_chan_out: float32 [768], replicated
The draws below stay inside these ranges and needn't reach their ends.
Inputs may be any that keep to these rules, and one draw needn't show every extreme that they name: counts[g, 0] is at most 12 and counts[g, 1] at most 2; some group has all its 224 px slots live and some group all its 384 px slots.
All inputs are finite; a program needn't handle non-finite values.
Results may differ from the reference program's by a relative error of at most 0.0071.
Values may be sent and summed in bfloat16 or wider, within the bound.
A program may use at most 192 MiB of HBM per device.

```python
import jax
import jax.numpy as jnp
from jax import lax

D = 768
FF = 3072
TOKEN_HIDDEN = 384
P_LO = 196
P_HI = 576
LO_SLOTS = 12
HI_SLOTS = 2
GROUPS = 8
IMG_LO = 96
IMG_HI = 16


def scaled_stream(key, base_values, shape_all):
    key_rows = jax.random.fold_in(key, 11)
    key_cols = jax.random.fold_in(key, 12)
    row_scale = jnp.exp(jax.random.uniform(key_rows, (shape_all[0], shape_all[1], 1), jnp.float32, -1.2, 1.2))
    col_scale = jnp.exp(jax.random.uniform(key_cols, (1, 1, shape_all[2]), jnp.float32, -1.2, 1.2))
    return base_values * row_scale * col_scale


def draw_x_lo(key, part):
    shape_all = (IMG_LO, P_LO, D)
    key_base = jax.random.fold_in(key, 10)
    base_values = jnp.clip(jax.random.normal(key_base, shape_all, jnp.float32), -4.0, 4.0)
    return scaled_stream(key, base_values, shape_all).astype(jnp.bfloat16)


def draw_x_hi(key, part):
    shape_all = (IMG_HI, P_HI, D)
    key_base = jax.random.fold_in(key, 20)
    base_values = jnp.clip(jax.random.normal(key_base, shape_all, jnp.float32), -4.0, 4.0)
    return scaled_stream(key, base_values, shape_all).astype(jnp.bfloat16)


def draw_counts(key, part):
    key_lo = jax.random.fold_in(key, 31)
    key_hi = jax.random.fold_in(key, 32)
    key_full_lo = jax.random.fold_in(key, 33)
    key_full_hi = jax.random.fold_in(key, 34)
    count_lo = jax.random.randint(key_lo, (GROUPS,), 1, LO_SLOTS + 1)
    count_hi = jax.random.randint(key_hi, (GROUPS,), 1, HI_SLOTS + 1)
    full_lo = jax.random.randint(key_full_lo, (), 0, GROUPS)
    full_hi = jax.random.randint(key_full_hi, (), 0, GROUPS)
    places = jnp.arange(GROUPS)
    count_lo = jnp.where(places == full_lo, LO_SLOTS, count_lo)
    count_hi = jnp.where(places == full_hi, HI_SLOTS, count_hi)
    return jnp.stack([count_lo, count_hi], axis=1).astype(jnp.int32)


def levels(key, shape, shards, low, high):
    factor_of, own = 1.0, jax.random.fold_in(key, 6)
    for position, parts in shards:
        steps = jnp.exp(jax.random.uniform(jax.random.fold_in(own, position), (parts,), jnp.float32, low / len(shards), high / len(shards)))
        factor_of = factor_of * jnp.repeat(steps, shape[position] // parts).reshape([-1 if axis == position else 1 for axis in range(len(shape))])
    return factor_of


def noise(stream_key, shape, scale, limit, pieces=(), dtype=jnp.bfloat16):
    loudness = levels(stream_key, shape, pieces, -0.22, 0.18) if pieces else 1.0
    values = jax.random.normal(stream_key, shape, jnp.float32) * scale * loudness
    return jnp.minimum(jnp.maximum(values, -limit), limit).astype(dtype)


def setup_inputs(seed: int = 0) -> dict:
    streams_of = jax.random.split(jax.random.key(seed), 22)
    x_lo = draw_x_lo(jax.random.fold_in(streams_of[21], 71), 0)
    x_hi = draw_x_hi(jax.random.fold_in(streams_of[21], 71), 0)
    cot_lo = noise(streams_of[2], (IMG_LO, P_LO, D), 1.0, 6.0, ((0, 8), (1, 4)))
    cot_hi = noise(streams_of[3], (IMG_HI, P_HI, D), 1.0, 6.0, ((0, 8), (1, 4)))
    counts = draw_counts(jax.random.fold_in(streams_of[21], 71), 0)
    ln1_gain = jnp.clip(1.0 + 0.18 * jax.random.normal(streams_of[5], (D,), jnp.float32), 0.099609375, 1.8984375).astype(jnp.bfloat16)
    ln1_bias = noise(streams_of[6], (D,), 0.5, 3.0)
    w_tok1_lo = noise(streams_of[7], (P_LO, TOKEN_HIDDEN), P_LO ** -0.5, 0.4375, ((1, 4),))
    b_tok1_lo = noise(streams_of[8], (TOKEN_HIDDEN,), 0.5, 3.0, ((0, 4),))
    w_tok2_lo = noise(streams_of[9], (TOKEN_HIDDEN, P_LO), TOKEN_HIDDEN ** -0.5, 0.3125, ((0, 4),))
    b_tok2_lo = noise(streams_of[10], (P_LO,), 0.5, 3.0, ((0, 4),))
    w_tok1_hi = noise(streams_of[11], (P_HI, TOKEN_HIDDEN), P_HI ** -0.5, 0.25, ((1, 4),))
    b_tok1_hi = noise(streams_of[12], (TOKEN_HIDDEN,), 0.5, 3.0, ((0, 4),))
    w_tok2_hi = noise(streams_of[13], (TOKEN_HIDDEN, P_HI), TOKEN_HIDDEN ** -0.5, 0.3125, ((0, 4),))
    b_tok2_hi = noise(streams_of[14], (P_HI,), 0.5, 3.0, ((0, 4),))
    ln2_gain = jnp.clip(1.0 + 0.18 * jax.random.normal(streams_of[15], (D,), jnp.float32), 0.099609375, 1.8984375).astype(jnp.bfloat16)
    ln2_bias = noise(streams_of[16], (D,), 0.5, 3.0)
    w_chan_in = noise(streams_of[17], (D, FF), D ** -0.5, 0.21875)
    b_chan_in = noise(streams_of[18], (FF,), 0.5, 3.0)
    w_chan_out = noise(streams_of[19], (FF, D), FF ** -0.5, 0.109375)
    b_chan_out = noise(streams_of[20], (D,), 0.5, 3.0)
    return dict(x_lo=x_lo, x_hi=x_hi, cot_lo=cot_lo, cot_hi=cot_hi, counts=counts, ln1_gain=ln1_gain, ln1_bias=ln1_bias, w_tok1_lo=w_tok1_lo, b_tok1_lo=b_tok1_lo, w_tok2_lo=w_tok2_lo, b_tok2_lo=b_tok2_lo, w_tok1_hi=w_tok1_hi, b_tok1_hi=b_tok1_hi, w_tok2_hi=w_tok2_hi, b_tok2_hi=b_tok2_hi, ln2_gain=ln2_gain, ln2_bias=ln2_bias, w_chan_in=w_chan_in, b_chan_in=b_chan_in, w_chan_out=w_chan_out, b_chan_out=b_chan_out)


EPS = 1e-06
exact_prec = lax.Precision.HIGHEST

@jax.custom_vjp
def low(v):
    return lax.optimization_barrier(v.astype(jnp.bfloat16)).astype(jnp.float32)

@jax.custom_vjp
def low_back(v):
    return v

def low_keep(v):
    return (low(v), None)

def low_pass(kept, grad):
    return (grad,)

def back_keep(v):
    return (v, None)

def back_low(kept, grad):
    return (low(grad),)
low.defvjp(low_keep, low_pass)
low_back.defvjp(back_keep, back_low)

def layer_norm(values, ln_gain, ln_shift):
    centre = values - lax.optimization_barrier(jnp.mean(values, axis=-1, keepdims=True))
    spread = lax.optimization_barrier(jnp.mean(centre * centre, axis=-1, keepdims=True))
    return centre * lax.rsqrt(spread + EPS) * ln_gain + ln_shift

def token_branch(normed, w_in, b_in, w_out, b_out):
    pre_token = jnp.einsum('npd,pk->nkd', normed, w_in, precision=exact_prec) + b_in[None, :, None]
    pre_token = low_back(pre_token)
    hid_token = low(jax.nn.gelu(pre_token))
    mixed = jnp.einsum('nkd,kp->npd', hid_token, w_out, precision=exact_prec) + b_out[None, :, None]
    return low_back(mixed)

def resolution_section(stream, shared, token_params):
    gain_one, shift_one, gain_two, shift_two, chan_w_in, chan_b_in, chan_w_out, chan_b_out = shared
    normed = low(layer_norm(stream, gain_one, shift_one))
    after_token = stream + token_branch(normed, token_params[0], token_params[1], token_params[2], token_params[3])
    normed_two = low(layer_norm(after_token, gain_two, shift_two))
    pre_chan = jnp.einsum('npd,df->npf', normed_two, chan_w_in, precision=exact_prec) + chan_b_in
    pre_chan = low_back(pre_chan)
    hid_chan = low(jax.nn.gelu(pre_chan))
    return after_token + jnp.einsum('npf,fd->npd', hid_chan, chan_w_out, precision=exact_prec) + chan_b_out

def group_forward(params, stream_lo, stream_hi):
    shared = (params[0], params[1], params[10], params[11], params[12], params[13], params[14], params[15])
    result_lo = resolution_section(stream_lo, shared, (params[2], params[3], params[4], params[5]))
    result_hi = resolution_section(stream_hi, shared, (params[6], params[7], params[8], params[9]))
    return (result_lo, result_hi)

def reference(x_lo, x_hi, cot_lo, cot_hi, counts, ln1_gain, ln1_bias, w_tok1_lo, b_tok1_lo, w_tok2_lo, b_tok2_lo, w_tok1_hi, b_tok1_hi, w_tok2_hi, b_tok2_hi, ln2_gain, ln2_bias, w_chan_in, b_chan_in, w_chan_out, b_chan_out):
    params = tuple((item.astype(jnp.float32) for item in (ln1_gain, ln1_bias, w_tok1_lo, b_tok1_lo, w_tok2_lo, b_tok2_lo, w_tok1_hi, b_tok1_hi, w_tok2_hi, b_tok2_hi, ln2_gain, ln2_bias, w_chan_in, b_chan_in, w_chan_out, b_chan_out)))
    groups = counts.shape[0]
    stream_lo = x_lo.astype(jnp.float32).reshape(groups, LO_SLOTS, P_LO, D)
    stream_hi = x_hi.astype(jnp.float32).reshape(groups, HI_SLOTS, P_HI, D)

    def forward(params_in, lo_in, hi_in):

        def one_group(pair_in):
            return group_forward(params_in, pair_in[0], pair_in[1])
        return lax.map(jax.checkpoint(one_group), (lo_in, hi_in))
    results, pullback = jax.vjp(forward, params, stream_lo, stream_hi)
    live_lo = (jnp.arange(LO_SLOTS)[None, :] < counts[:, 0:1]).astype(jnp.float32)[:, :, None, None]
    live_hi = (jnp.arange(HI_SLOTS)[None, :] < counts[:, 1:2]).astype(jnp.float32)[:, :, None, None]
    cot_live_lo = cot_lo.astype(jnp.float32).reshape(groups, LO_SLOTS, P_LO, D) * live_lo
    cot_live_hi = cot_hi.astype(jnp.float32).reshape(groups, HI_SLOTS, P_HI, D) * live_hi
    gradients, grad_lo, grad_hi = pullback((cot_live_lo, cot_live_hi))
    out_lo = (results[0] * live_lo).astype(jnp.bfloat16).reshape(groups * LO_SLOTS, P_LO, D)
    out_hi = (results[1] * live_hi).astype(jnp.bfloat16).reshape(groups * HI_SLOTS, P_HI, D)
    return (out_lo, out_hi, grad_lo.reshape(groups * LO_SLOTS, P_LO, D), grad_hi.reshape(groups * HI_SLOTS, P_HI, D), gradients[0], gradients[1], gradients[2], gradients[3], gradients[4], gradients[5], gradients[6], gradients[7], gradients[8], gradients[9], gradients[10], gradients[11], gradients[12], gradients[13], gradients[14], gradients[15])
```

```python
import functools

import jax
import jax.numpy as jnp
from jax import lax
from jax.experimental import pallas as pl
from jax.experimental.pallas import tpu as pltpu
from jax.sharding import PartitionSpec as P

MESH = pl.DeviceIdType.MESH
EPS = 1e-06
GELU_A, GELU_B = 0.7978845608028654, 0.044715
f32, bf16 = jnp.float32, jnp.bfloat16

LINE, PAIR = 4, 2
SHARDS = 16
LAND = {"xzy": dict(x=(0, 8), z=(8, 10), y=(18, 1)),
        "yzx": dict(y=(0, 8), z=(8, 10), x=(18, 1))}
LANDED = 19
NSEM = 10


class Place:
    def __init__(self):
        dp, mp = lax.axis_index("dp"), lax.axis_index("mp")
        self.block = dp // (LINE * PAIR)
        self.z = (dp // PAIR) % LINE
        self.x = dp % PAIR
        self.y = mp // 2
        self.c = mp % 2

    def at(self, z=None, x=None, y=None, c=None):
        z = self.z if z is None else z
        x = self.x if x is None else x
        y = self.y if y is None else y
        c = self.c if c is None else c
        return (self.block * (LINE * PAIR) + z * PAIR + x, y * 2 + c)

    def up(self):
        return self.at(z=jnp.minimum(self.z + 1, LINE - 1))

    def down(self):
        return self.at(z=jnp.maximum(self.z - 1, 0))

    def pair(self, axis):
        return self.at(**{axis: 1 - getattr(self, axis)})


def add_into(ref, idx, *others):
    total = ref[idx].astype(f32)
    for o in others:
        total = total + o.astype(f32)
    ref[idx] = total.astype(bf16)


class AllReduce:
    def __init__(self, place, g, land_core, land, out, send, recv, kept):
        self.p, self.g, self.lc, self.l, self.out, self.send, self.recv, self.kept = place, g, land_core, land, out, send, recv, kept
        self.unit = g.shape[1] // (2 * SHARDS)

    def sh(self, start, n):
        if isinstance(start, int):
            return pl.ds(start * self.unit, n * self.unit)
        return pl.ds(pl.multiple_of(start * self.unit, 16), n * self.unit)

    def copy(self, f, k, src, dst, dev):
        return pltpu.make_async_remote_copy(src, dst, self.send.at[f, k], self.recv.at[f, k], device_id=dev, device_id_type=MESH)

    def half(self, f, start, n):
        return self.g.at[f, self.sh(self.p.c * SHARDS + start, n)]

    def core(self, f):
        p = self.p
        return [self.copy(f, 0, self.g.at[f, self.sh((1 - p.c) * SHARDS, SHARDS)], self.lc.at[f % self.lc.shape[0]], p.pair("c"))]

    def core_add(self, f):
        add_into(self.g, (f, self.sh(self.p.c * SHARDS, SHARDS)), self.lc[f % self.lc.shape[0]])

    def regions(self, path):
        base, n, out = 0, SHARDS, {}
        for axis in path:
            out[axis] = (base, n)
            parts = LINE if axis == "z" else PAIR
            n = n // parts
            base = base + getattr(self.p, axis) * n
        out["end"] = (base, n)
        return out

    def pair_send(self, f, path, axis):
        base, n = self.regions(path)[axis]
        other = 1 - getattr(self.p, axis)
        off, m = LAND[path][axis]
        k = {"x": 1, "y": 2}[axis]
        return [self.copy(f, k, self.half(f, base + other * (n // 2), n // 2), self.l.at[f, self.sh(off, m)], self.p.pair(axis))]

    def pair_add(self, f, path, axis):
        base, n = self.regions(path)[axis]
        off, m = LAND[path][axis]
        s = self.p.c * SHARDS + base + getattr(self.p, axis) * m
        add_into(self.g, (f, self.sh(s, m)), self.l[f, self.sh(off, m)])

    def z_copies(self, f, path, k, back):
        base, n = self.regions(path)["z"]
        m = n // LINE
        off, _ = LAND[path]["z"]
        z = self.p.z
        if back:
            up, down = self.done(f, base, k * m), self.done(f, base + (LINE - k) * m, k * m)
            up = self.copy(f, 7, up, up, self.p.up())
            down = self.copy(f, 8, down, down, self.p.down())
        else:
            w = (LINE - k) * m
            up = self.copy(f, 3, self.half(f, base + k * m, w), self.l.at[f, self.sh(off, w)], self.p.up())
            down = self.copy(f, 4, self.half(f, base, w), self.l.at[f, self.sh(off + (k + 1) * m, w)], self.p.down())
        return [(z == k - 1, z == k, up), (z == LINE - k, z == LINE - 1 - k, down)]

    def z_add(self, f, path, k):
        base, n = self.regions(path)["z"]
        m = n // LINE
        off, _ = LAND[path]["z"]
        c0 = self.p.c * SHARDS + base
        w = (LINE - k) * m

        @pl.when(self.p.z == k)
        def _():
            add_into(self.g, (f, self.sh(c0 + k * m, w)), self.l[f, self.sh(off, w)])

        @pl.when(self.p.z == LINE - 1 - k)
        def _():
            add_into(self.g, (f, self.sh(c0, w)), self.l[f, self.sh(off + (k + 1) * m, w)])

    def done(self, f, start, n):
        return self.out.at[f, self.sh(self.p.c * SHARDS + start, n)]

    def same(self, f, k, start, n, dev):
        ref = self.done(f, start, n)
        return self.copy(f, k, ref, ref, dev)

    def pair_back(self, f, path, axis):
        base, n = self.regions(path)[axis]
        k = {"x": 5, "y": 6}[axis]
        if axis == path[-1]:
            at, ref = self.regions(path)["end"]
            src, dst = self.half(f, at, ref), self.done(f, at, ref)
            return [self.copy(f, k, src, dst, self.p.pair(axis)), pltpu.make_async_copy(src, dst, self.kept.at[f])]
        return [self.same(f, k, base + getattr(self.p, axis) * (n // 2), n // 2, self.p.pair(axis))]

    def core_back(self, f):
        return [self.same(f, 9, 0, SHARDS, self.p.pair("c"))]

    def steps(self, path):
        seq = [(self.core, self.core_add)]
        for axis in path:
            if axis == "z":
                for k in range(1, LINE):
                    seq.append((functools.partial(self.z_copies, path=path, k=k, back=False), functools.partial(self.z_add, path=path, k=k)))
            else:
                seq.append((functools.partial(self.pair_send, path=path, axis=axis), functools.partial(self.pair_add, path=path, axis=axis)))
        for axis in path[::-1]:
            if axis == "z":
                for k in range(1, LINE):
                    seq.append((functools.partial(self.z_copies, path=path, k=k, back=True), None))
            else:
                seq.append((functools.partial(self.pair_back, path=path, axis=axis), None))
        seq.append((self.core_back, None))
        return seq

    def run_stage(self, f, s, path):
        seq = self.steps(path)
        if s > 0:
            copies, add = seq[s - 1]
            for cp in copies(f):
                if isinstance(cp, tuple):
                    sends, gets, one = cp
                    pl.when(sends)(one.wait_send)
                    pl.when(gets)(one.wait_recv)
                else:
                    cp.wait()
            if add is not None:
                add(f)
        if s < len(seq):
            for cp in seq[s][0](f):
                if isinstance(cp, tuple):
                    pl.when(cp[0])(cp[2].start)
                else:
                    cp.start()

    def stages(self, path):
        return len(self.steps(path)) + 1

    def step(self, i, last, paths, skew):
        n = self.stages(paths[0])
        for s in range(n - 1, -1, -1):
            f = i - s * skew

            def go(f=f, s=s):
                if s in (0, n - 1):
                    self.run_stage(f, s, paths[0])
                    return
                for core, path in enumerate(paths):
                    @pl.when(self.p.c == core)
                    def _():
                        self.run_stage(f, s, path)
            pl.when((f >= 0) & (f < last))(go)


PATHS = ("xzy", "yzx")
SKEW = 2
CHUNK = 256
SMALL = 16


def mm(a, b, ca=1, cb=0):
    return lax.dot_general(a, b, (((ca,), (cb,)), ((), ())), preferred_element_type=f32)


def gelu(v):
    return v * (0.5 * (1.0 + jnp.tanh(GELU_A * v * (1.0 + GELU_B * (v * v)))))


def gelu_both(v):
    sq = v * v
    t = jnp.tanh(GELU_A * v * (1.0 + GELU_B * sq))
    h = 0.5 * (1.0 + t)
    return v * h, h + 0.5 * v * (1.0 - t * t) * (GELU_A * (1.0 + 3.0 * GELU_B * sq))


def centred(v):
    c = v - jnp.mean(v, -1, keepdims=True)
    return c, lax.rsqrt(jnp.mean(c * c, -1, keepdims=True) + EPS)


def norm_back(c, rs, u):
    xh = c * rs
    return (u - jnp.mean(u, -1, keepdims=True) - xh * jnp.mean(u * xh, -1, keepdims=True)) * rs


def colsum(v):
    return jnp.sum(v, 0, keepdims=True)


def up16(n):
    return -(-n // 16) * 16


def up128(n):
    return -(-n // 128) * 128


class Sizes:
    def __init__(self, x_lo, x_hi, w_tok1_lo, w_chan_in):
        self.slots, self.q, self.d = x_lo.shape
        self.imgs = self.slots // 4
        self.qh = x_hi.shape[1]
        self.p, self.ph = 4 * self.q, 4 * self.qh
        self.ks = w_tok1_lo.shape[1]
        self.k = 4 * self.ks
        self.ff = w_chan_in.shape[1]
        self.chunks = self.ff // CHUNK
        self.pr = up16(self.p)
        self.own = 2 * self.qh
        self.hi0 = self.imgs * self.pr
        self.rows = self.hi0 + self.own
        self.wl, self.wh = up128(self.p), up128(self.ph)
        self.lanes = 2 * self.wl + 2 * self.wh + 256
        self.half_rows = CHUNK * (self.d // 256)
        self.t_lo = 3 * self.own
        self.t_rows = -(-(self.t_lo + self.k) // (16 * SHARDS)) * (16 * SHARDS)


def kernel(
    S,
    x_lo, x_hi, cot_lo, cot_hi, counts, wpack, bias_lo, bias_hi, w_in, w_out, b_in, b_out, gain1, shift1, gain2, shift2,
    out_lo, out_hi, grad_lo, grad_hi, g_sum, t_sum, s_sum,
    xl, xh, cl, ch, wg, bl, bh, w2t_lo, w1_lo, w2t_hi, w1_hi, bcol, af, nb, nh, n2, ct, tmp, gmh, hid, gp, winv, woutv,
    g, g_core, g_land, t, t_core, t_land, gw1, gw2, gb, sv, s1, s2,
    lo_send, lo_recv, hi_send, hi_recv, w_send, w_recv, ring_send, ring_recv, g_send, g_recv, t_send, t_recv,
    s_send, s_recv, local, g_kept, t_kept,
):
    p = Place()
    y, c = p.y, p.c
    m = y * 2 + c
    dpi = p.z * PAIR + p.x
    peers = [(y, 1 - c), (1 - y, c), (1 - y, 1 - c)]
    d = S.d

    def dev(yy, cc):
        return p.at(y=yy, c=cc)

    def rcopy(src, dst, send, recv, to):
        return pltpu.make_async_remote_copy(src, dst, send, recv, device_id=to, device_id_type=MESH)

    def dp_dev(k):
        i = (dpi + k) % (LINE * PAIR)
        return p.at(z=i // PAIR, x=i % PAIR)

    sem = pltpu.get_barrier_semaphore()
    for yy, cc in peers:
        pl.semaphore_signal(sem, inc=1, device_id=dev(yy, cc), device_id_type=MESH)
    for k in range(1, LINE * PAIR):
        pl.semaphore_signal(sem, inc=1, device_id=dp_dev(k), device_id_type=MESH)
    pl.semaphore_wait(sem, 3 + LINE * PAIR - 1)

    def lo_out(kind, i, src, dst):
        res = []
        for j, (yy, cc) in enumerate(peers):
            mm_ = yy * 2 + cc
            res.append(rcopy(src.at[S.imgs * mm_ + i], dst.at[m, i], lo_send.at[kind, j, i], lo_recv.at[kind, m, i], dev(yy, cc)))
        return res

    def lo_in(kind, i, dst):
        return [rcopy(dst.at[yy * 2 + cc, i], dst.at[yy * 2 + cc, i], lo_send.at[kind, j, i], lo_recv.at[kind, yy * 2 + cc, i], dev(yy, cc)) for j, (yy, cc) in enumerate(peers)]

    def lo_local(kind, i, src, dst):
        return pltpu.make_async_copy(src.at[S.imgs * m + i], dst.at[m, i], local.at[kind, i])

    def lo_back(kind, i, src, dst):
        return [rcopy(src.at[yy * 2 + cc, i], dst.at[S.imgs * m + i], lo_send.at[kind, j, i], lo_recv.at[kind, m, i], dev(yy, cc)) for j, (yy, cc) in enumerate(peers)]

    def lo_back_in(kind, i, dst):
        return [rcopy(dst.at[S.imgs * (yy * 2 + cc) + i], dst.at[S.imgs * (yy * 2 + cc) + i], lo_send.at[kind, j, i], lo_recv.at[kind, yy * 2 + cc, i], dev(yy, cc)) for j, (yy, cc) in enumerate(peers)]

    def lo_back_local(kind, i, src, dst):
        return pltpu.make_async_copy(src.at[m, i], dst.at[S.imgs * m + i], local.at[kind, i])

    def hi_out(kind, src, dst):
        res = []
        for h in range(2):
            mine = (y == h) & (c == y)
            ref = src.at[h] if src.shape[0] == 2 and len(src.shape) == 3 else src
            res.append((mine, rcopy(ref, dst.at[c], hi_send.at[kind, h], hi_recv.at[kind, c], dev(h, y)),
                        pltpu.make_async_copy(ref, dst.at[c], local.at[kind, S.imgs])))
        return res

    def hi_in(kind, dst):
        res = []
        for j in range(2):
            mine = (y == c) & (c == j)
            res.append((mine, rcopy(dst.at[j], dst.at[j], hi_send.at[kind, j], hi_recv.at[kind, j], dev(c, j))))
        return res

    def hi_back(kind, src, dst):
        res = []
        for j in range(2):
            mine = (y == c) & (c == j)
            res.append((mine, rcopy(src.at[j], dst.at[y], hi_send.at[kind, j], hi_recv.at[kind, y], dev(c, j)),
                        pltpu.make_async_copy(src.at[j], dst.at[y], local.at[kind, S.imgs])))
        return res

    def hi_back_in(kind, dst):
        res = []
        for h in range(2):
            mine = (y == h) & (c == y)
            res.append((mine, rcopy(dst.at[h], dst.at[h], hi_send.at[kind, h], hi_recv.at[kind, h], dev(h, y))))
        return res

    def start(copies):
        for cp in copies:
            cp.start()

    def start_hi(copies):
        for mine, remote, here in copies:
            pl.when(mine)(here.start)
            pl.when(jnp.logical_not(mine))(remote.start)

    def sent_hi(copies):
        for mine, remote, here in copies:
            pl.when(mine)(here.wait)
            pl.when(jnp.logical_not(mine))(remote.wait_send)

    def got_hi(copies):
        for mine, remote in copies:
            pl.when(jnp.logical_not(mine))(remote.wait_recv)

    my = (1 - y) * 2 + c
    w_own = pltpu.make_async_copy(wpack, wg.at[m], local.at[4, 0])
    w_y = rcopy(wpack, wg.at[m], w_send.at[0], w_recv.at[0], dev(1 - y, c))
    w_c = rcopy(wpack, wg.at[m], w_send.at[1], w_recv.at[1], dev(y, 1 - c))
    w_f = rcopy(wg.at[my], wg.at[my], w_send.at[2], w_recv.at[2], dev(y, 1 - c))
    w_own.start()
    w_y.start()
    w_c.start()
    start_hi(hi_out(0, x_hi, xh))
    bias_out = [rcopy(bias_lo, bl.at[m], w_send.at[3 + j], w_recv.at[3 + m], dev(yy, cc)) for j, (yy, cc) in enumerate(peers)]
    start(bias_out)
    bl[m] = bias_lo[...]
    bias_hi_out = hi_out(4, bias_hi, bh)
    start_hi(bias_hi_out)
    for i in range(S.imgs):
        start(lo_out(0, i, x_lo, xl))
        lo_local(0, i, x_lo, xl).start()
    start_hi(hi_out(1, cot_hi, ch))
    for i in range(S.imgs):
        start(lo_out(1, i, cot_lo, cl))
        lo_local(1, i, cot_lo, cl).start()
    load_in = pltpu.make_async_copy(w_in, winv, local.at[4, 1])
    load_out = pltpu.make_async_copy(w_out, woutv, local.at[4, 2])
    load_in.start()
    load_out.start()

    gv1, sv1 = gain1[...].astype(f32), shift1[...].astype(f32)
    gv2, sv2 = gain2[...].astype(f32), shift2[...].astype(f32)
    hi = pl.ds(S.hi0, S.own)
    own = pl.ds(pl.multiple_of(c * S.own, 16), S.own)

    def img(i):
        return pl.ds(pl.multiple_of(i * S.pr, 16), S.pr)

    def gather_rows(block, i):
        for s in range(4):
            tmp[s * S.q:(s + 1) * S.q, :] = block[s, i].astype(f32)
        if S.pr > S.p:
            tmp[S.p:S.pr, :] = jnp.zeros((S.pr - S.p, d), f32)

    def scatter_rows(block, i):
        for s in range(4):
            block[s, i] = tmp[s * S.q:(s + 1) * S.q, :].astype(bf16)

    sv[...] = jnp.zeros_like(sv)
    t[...] = jnp.zeros_like(t)
    gw1[...] = jnp.zeros_like(gw1)
    gw2[...] = jnp.zeros_like(gw2)

    got_hi(hi_in(0, xh))
    sent_hi(hi_out(0, x_hi, xh))
    v = xh[...].reshape(S.own, d).astype(f32)
    cen, rs = centred(v)
    n = (cen * rs * gv1 + sv1).astype(bf16)
    nb[hi, :] = n
    nh[own, :] = n
    af[hi, :] = v
    nh_copy = rcopy(nh.at[own], nh.at[own], ring_send.at[0], ring_recv.at[0], dev(y, 1 - c))
    nh_copy.start()

    w_own.wait()
    w_y.wait()
    w_f.start()
    w_c.wait()
    w_f.wait()
    o1, o2, o3, o4 = S.wl, 2 * S.wl, 2 * S.wl + S.wh, 2 * S.wl + 2 * S.wh

    def w1t_lo():
        return wg[:, :, 0:S.pr].reshape(S.k, S.pr)

    def w2_lo():
        return wg[:, :, o1:o1 + S.pr].reshape(S.k, S.pr)

    def w1t_hi():
        return wg[:, :, o2:o2 + S.ph].reshape(S.k, S.ph)

    def w2_hi():
        return wg[:, :, o3:o3 + S.ph].reshape(S.k, S.ph)

    def b1_lo():
        return wg[:, :, o4:o4 + 128].reshape(S.k, 128).astype(f32)[:, 0:1]

    def b1_hi():
        return wg[:, :, o4 + 128:o4 + 256].reshape(S.k, 128).astype(f32)[:, 0:1]

    w1_lo[...] = w1t_lo().T
    w2t_lo[...] = w2_lo().T
    w1_hi[...] = w1t_hi().T
    w2t_hi[...] = w2_hi().T
    for j, (yy, cc) in enumerate(peers):
        bias_out[j].wait_send()
        s = yy * 2 + cc
        rcopy(bl.at[s], bl.at[s], w_send.at[3 + j], w_recv.at[3 + s], dev(yy, cc)).wait_recv()
    got_hi(hi_in(4, bh))
    sent_hi(bias_hi_out)
    bcol[...] = jnp.zeros_like(bcol)
    for s in range(4):
        bcol[s * S.q:(s + 1) * S.q, :] = bl[s].astype(f32)

    def fwd_lo(i, carry):
        for cp in lo_in(0, i, xl):
            cp.wait_recv()
        lo_local(0, i, x_lo, xl).wait()
        gather_rows(xl, i)
        v = tmp[...]
        cen, rs = centred(v)
        n = (cen * rs * gv1 + sv1).astype(bf16)
        nb[img(i), :] = n
        ht = gelu(mm(w1t_lo(), n) + b1_lo()).astype(bf16)
        af[img(i), :] = v + (mm(w2t_lo[...], ht) + bcol[:, 0:1])
        return carry

    lax.fori_loop(0, S.imgs, fwd_lo, 0)
    nh_copy.wait()
    ht = gelu(mm(w1t_hi(), nh[...]) + b1_hi()).astype(bf16)
    bcol_hi = bh[...].reshape(S.own, 128).astype(f32)[:, 0:1]
    af[hi, :] = af[hi, :] + (mm(w2t_hi[own, :], ht) + bcol_hi)

    def norm_two(rows):
        cen, rs = centred(af[rows, :])
        n2[rows, :] = (cen * rs * gv2 + sv2).astype(bf16)

    norm_two(hi)

    def norm_lo(i, carry):
        norm_two(img(i))
        return carry

    lax.fori_loop(0, S.imgs, norm_lo, 0)

    def live_lo(i):
        return jnp.where(S.imgs * m + i < counts[0, 0], 1.0, 0.0).astype(f32)

    live_hi = jnp.where(y < counts[0, 1], 1.0, 0.0).astype(f32)
    got_hi(hi_in(1, ch))
    sent_hi(hi_out(1, cot_hi, ch))
    ct[hi, :] = (ch[...].reshape(S.own, d).astype(f32) * live_hi).astype(bf16)

    def cot_rows(i, carry):
        for cp in lo_in(1, i, cl):
            cp.wait_recv()
        lo_local(1, i, cot_lo, cl).wait()
        gather_rows(cl, i)
        ct[img(i), :] = (tmp[...] * live_lo(i)).astype(bf16)
        return carry

    lax.fori_loop(0, S.imgs, cot_rows, 0)
    for kind, src, dst in ((0, x_lo, xl), (1, cot_lo, cl)):
        for i in range(S.imgs):
            for cp in lo_out(kind, i, src, dst):
                cp.wait_send()
    load_in.wait()
    load_out.wait()

    def channel(f):
        cols = pl.ds(pl.multiple_of(f * CHUNK, CHUNK), CHUNK)
        h, slope = gelu_both(mm(n2[...], winv[:, cols]) + b_in[:, cols].astype(f32))
        hb = h.astype(bf16)
        hid[:, cols] = hb
        gpre = (mm(ct[...], woutv[cols, :], 1, 1) * slope).astype(bf16)
        gp[:, cols] = gpre
        gb[:, cols] = colsum(gpre.astype(f32))
        g[f, 0:d, :] = mm(n2[...], gpre, 0, 0).astype(bf16)
        grad = mm(hb, ct[...], 0, 0)
        for j in range(d // 256):
            g[f, S.half_rows + CHUNK * j:S.half_rows + CHUNK * (j + 1), :] = grad[:, 256 * j:256 * (j + 1)].astype(bf16)

    bo = b_out[...].astype(f32)

    def channel_back(rows, live):
        a = af[rows, :]
        out = (a + mm(hid[rows, :], woutv[...]) + bo) * live
        gn = mm(gp[rows, :], winv[...], 1, 1)
        cen, rs = centred(a)
        c_rows = ct[rows, :].astype(f32)
        grad = c_rows + norm_back(cen, rs, gn * gv2)
        sv[0:1, :] += colsum(c_rows)
        sv[1:2, :] += colsum(gn * (cen * rs))
        sv[2:3, :] += colsum(gn)
        af[rows, :] = grad
        n2[rows, :] = grad.astype(bf16)
        return out

    def back_hi():
        out = channel_back(hi, live_hi)
        ch[...] = out.astype(bf16).reshape(2, S.qh, d)
        start_hi(hi_back(2, ch, out_hi))
        gmh[own, :] = n2[hi, :]
        gm_copy.start()

    gm_copy = rcopy(gmh.at[own], gmh.at[own], ring_send.at[1], ring_recv.at[1], dev(y, 1 - c))

    def back_lo(i):
        tmp[...] = channel_back(img(i), live_lo(i))
        scatter_rows(cl, i)
        start(lo_back(2, i, cl, out_lo))
        lo_back_local(2, i, cl, out_lo).start()

    ones = jnp.ones((8, d), bf16)

    def first_norm_back(v, gn, rows):
        cen, rs = centred(v)
        sv[3:4, :] += colsum(gn * (cen * rs))
        sv[4:5, :] += colsum(gn)
        return af[rows, :] + norm_back(cen, rs, gn * gv1)

    def token_lo(i):
        n = nb[img(i), :]
        gm = n2[img(i), :]
        h, slope = gelu_both(mm(w1t_lo(), n) + b1_lo())
        gw2[:, 0:S.pr] += mm(h.astype(bf16), gm, 1, 1)
        gpt = (mm(w2_lo(), gm) * slope).astype(bf16)
        gw1[:, 0:S.pr] += mm(gpt, n, 1, 1)
        sv[9:10, 0:S.k] += mm(ones, gpt, 1, 1)[0:1]
        sv[10:11, 0:S.pr] += mm(ones, gm, 1, 1)[0:1]
        gn = mm(w1_lo[...], gpt)
        gather_rows(xl, i)
        tmp[...] = first_norm_back(tmp[...], gn, img(i))
        scatter_rows(xl, i)
        start(lo_back(3, i, xl, grad_lo))
        lo_back_local(3, i, xl, grad_lo).start()

    def token_hi():
        gm_copy.wait()
        n = nb[hi, :]
        gm = n2[hi, :]
        h, slope = gelu_both(mm(w1t_hi(), nh[...]) + b1_hi())
        ga2 = mm(gm, h.astype(bf16), 1, 1)
        gpt = (mm(w2_hi(), gmh[...]) * slope).astype(bf16)
        ga1 = mm(n, gpt, 1, 1)
        once = jnp.where(c == 0, 1.0, 0.0).astype(f32)
        sv[11:12, 0:S.k] += mm(ones, gpt, 1, 1)[0:1] * once
        sv[pl.ds(12 + c, 1), 0:S.own] = mm(ones, gm, 1, 1)[0:1]
        gn = mm(w1_hi[own, :], gpt)
        grad = first_norm_back(xh[...].reshape(S.own, d).astype(f32), gn, hi)
        xh[...] = grad.astype(bf16).reshape(2, S.qh, d)
        start_hi(hi_back(3, xh, grad_hi))
        for j in range(S.ff // d):
            sv[5 + j:6 + j, :] = gb[:, d * j:d * (j + 1)]
        for k in range(2):
            @pl.when(c == k)
            def _():
                t[0, S.t_rows * k:S.t_rows * k + S.own, :] = ga1[:, 0:256].astype(bf16)
                t[0, S.t_rows * k + S.own:S.t_rows * k + 2 * S.own, :] = ga2[:, 0:256].astype(bf16)
                t[0, S.t_rows * k + 2 * S.own:S.t_rows * k + 3 * S.own, 0:128] = ga1[:, 256:384].astype(bf16)
                t[0, S.t_rows * k + 2 * S.own:S.t_rows * k + 3 * S.own, 128:256] = ga2[:, 256:384].astype(bf16)
        t[0, S.t_lo:S.t_lo + S.k, :] = gw1[...].astype(bf16)
        t[0, S.t_rows + S.t_lo:S.t_rows + S.t_lo + S.k, :] = gw2[...].astype(bf16)
        s1[m] = sv[...]
        start(s1_out)

    s1_out = [rcopy(s1.at[m], s1.at[m], s_send.at[j], s_recv.at[m], dev(yy, cc)) for j, (yy, cc) in enumerate(peers)]
    s2_out = [rcopy(s2.at[dpi], s2.at[dpi], s_send.at[3 + k], s_recv.at[4 + dpi], dp_dev(k)) for k in range(1, LINE * PAIR)]

    ar = AllReduce(p, g, g_core, g_land, g_sum, g_send, g_recv, g_kept)
    art = AllReduce(p, t, t_core, t_land, t_sum, t_send, t_recv, t_kept)
    stages = ar.stages(PATHS[0])
    nc = S.chunks
    b0 = nc + 1 + S.imgs
    t0 = b0 + S.imgs

    def step(i, carry):
        pl.when(i < nc)(lambda: channel(i))
        pl.when(i == nc)(back_hi)
        pl.when((i > nc) & (i < b0))(lambda: back_lo(i - nc - 1))
        pl.when((i >= b0) & (i < t0))(lambda: token_lo(i - b0))
        pl.when(i == t0)(token_hi)
        ar.step(i, nc, PATHS, SKEW)
        art.step(i - t0, 1, PATHS, 1)
        return carry

    lax.fori_loop(0, max(nc + (stages - 1) * SKEW, t0 + stages), step, 0)

    for j, (yy, cc) in enumerate(peers):
        s = yy * 2 + cc
        s1_out[j].wait_send()
        rcopy(s1.at[s], s1.at[s], s_send.at[j], s_recv.at[s], dev(yy, cc)).wait_recv()
    s2[dpi] = s1[0] + s1[1] + s1[2] + s1[3]
    start(s2_out)
    for k in range(1, LINE * PAIR):
        i = (dpi + k) % (LINE * PAIR)
        s2_out[k - 1].wait_send()
        rcopy(s2.at[i], s2.at[i], s_send.at[3 + k], s_recv.at[4 + i], dp_dev(k)).wait_recv()
    total = s2[0]
    for i in range(1, LINE * PAIR):
        total = total + s2[i]
    s_sum[...] = total

    for kind, src, src_hi, dst, dst_hi in ((2, cl, ch, out_lo, out_hi), (3, xl, xh, grad_lo, grad_hi)):
        for i in range(S.imgs):
            for cp in lo_back(kind, i, src, dst):
                cp.wait_send()
            for cp in lo_back_in(kind, i, dst):
                cp.wait_recv()
            lo_back_local(kind, i, src, dst).wait()
        sent_hi(hi_back(kind, src_hi, dst_hi))
        got_hi(hi_back_in(kind, dst_hi))


def mixer(S, args):
    V = pl.BlockSpec(memory_space=pltpu.VMEM)
    A = pl.BlockSpec(memory_space=pl.ANY)
    M = pl.BlockSpec(memory_space=pltpu.SMEM)
    sds = jax.ShapeDtypeStruct
    d, dma = S.d, pltpu.SemaphoreType.DMA
    nc = S.chunks
    unit = 2 * S.half_rows // (2 * SHARDS)
    tu = S.t_rows // SHARDS
    scratch = [
        pltpu.VMEM((4, S.imgs, S.q, d), bf16), pltpu.VMEM((2, S.qh, d), bf16),
        pltpu.VMEM((4, S.imgs, S.q, d), bf16), pltpu.VMEM((2, S.qh, d), bf16),
        pltpu.VMEM((4, S.ks, S.lanes), bf16), pltpu.VMEM((4, S.q, 128), bf16), pltpu.VMEM((2, S.qh, 128), bf16),
        pltpu.VMEM((S.pr, S.k), bf16), pltpu.VMEM((S.pr, S.k), bf16), pltpu.VMEM((S.ph, S.k), bf16), pltpu.VMEM((S.ph, S.k), bf16),
        pltpu.VMEM((S.pr, 128), f32),
        pltpu.VMEM((S.rows, d), f32), pltpu.VMEM((S.rows, d), bf16), pltpu.VMEM((S.ph, d), bf16), pltpu.VMEM((S.rows, d), bf16),
        pltpu.VMEM((S.rows, d), bf16), pltpu.VMEM((S.pr, d), f32), pltpu.VMEM((S.ph, d), bf16),
        pltpu.VMEM((S.rows, S.ff), bf16), pltpu.VMEM((S.rows, S.ff), bf16), pltpu.VMEM((d, S.ff), bf16), pltpu.VMEM((S.ff, d), bf16),
        pltpu.VMEM((nc, 2 * SHARDS * unit, 256), bf16), pltpu.VMEM((2 * SKEW, SHARDS * unit, 256), bf16), pltpu.VMEM((nc, LANDED * unit, 256), bf16),
        pltpu.VMEM((1, 2 * S.t_rows, 256), bf16), pltpu.VMEM((1, S.t_rows, 256), bf16), pltpu.VMEM((1, LANDED * tu, 256), bf16),
        pltpu.VMEM((S.k, 256), f32), pltpu.VMEM((S.k, 256), f32), pltpu.VMEM((1, S.ff), f32),
        pltpu.VMEM((SMALL, d), f32), pltpu.VMEM((4, SMALL, d), f32), pltpu.VMEM((LINE * PAIR, SMALL, d), f32),
        dma((4, 3, S.imgs)), dma((4, 4, S.imgs)), dma((5, 2)), dma((5, 2)), dma((6,)), dma((7,)), dma((2,)), dma((2,)),
        dma((nc, NSEM)), dma((nc, NSEM)), dma((1, NSEM)), dma((1, NSEM)), dma((11,)), dma((12,)), dma((5, S.imgs + 1)), dma((nc,)), dma((1,)),
    ]
    return pl.pallas_call(
        functools.partial(kernel, S),
        out_shape=(
            sds((S.slots, S.q, d), bf16), sds((2, S.qh, d), bf16), sds((S.slots, S.q, d), bf16), sds((2, S.qh, d), bf16),
            sds((nc, 2 * S.half_rows, 256), bf16), sds((1, 2 * S.t_rows, 256), bf16), sds((SMALL, d), f32),
        ),
        in_specs=[A, A, A, A, M, A, V, V, A, A, V, V, V, V, V, V],
        out_specs=(A, A, A, A, A, A, V),
        scratch_shapes=scratch,
        compiler_params=pltpu.CompilerParams(collective_id=0, has_side_effects=True, vmem_limit_bytes=63 * 1024 * 1024),
    )(*args)


def widen(S, g):
    d = S.d

    def place(g_ref, in_ref, out_ref):
        in_ref[...] = g_ref[0, 0:d, :].astype(f32)
        for j in range(d // 256):
            out_ref[:, 256 * j:256 * (j + 1)] = g_ref[0, S.half_rows + CHUNK * j:S.half_rows + CHUNK * (j + 1), :].astype(f32)

    return pl.pallas_call(
        place,
        grid=(S.chunks,),
        out_shape=(jax.ShapeDtypeStruct((d, S.ff), f32), jax.ShapeDtypeStruct((S.ff, d), f32)),
        in_specs=[pl.BlockSpec((1, 2 * S.half_rows, 256), lambda i: (i, 0, 0))],
        out_specs=(pl.BlockSpec((d, CHUNK), lambda i: (0, i)), pl.BlockSpec((CHUNK, d), lambda i: (i, 0))),
    )(g)


def body(
    groups,
    x_lo, x_hi, cot_lo, cot_hi, counts, ln1_gain, ln1_bias, w_tok1_lo, b_tok1_lo, w_tok2_lo, b_tok2_lo, w_tok1_hi, b_tok1_hi,
    w_tok2_hi, b_tok2_hi, ln2_gain, ln2_bias, w_chan_in, b_chan_in, w_chan_out, b_chan_out,
):
    S = Sizes(x_lo, x_hi, w_tok1_lo, w_chan_in)

    def lanes(w, n):
        return jnp.pad(w, ((0, 0), (0, n - w.shape[1])))

    def column(b):
        return jnp.broadcast_to(b[:, None], (b.shape[0], 128))

    wpack = jnp.concatenate(
        [lanes(w_tok1_lo.T, S.wl), lanes(w_tok2_lo, S.wl), lanes(w_tok1_hi.T, S.wh), lanes(w_tok2_hi, S.wh), column(b_tok1_lo), column(b_tok1_hi)],
        axis=1,
    )
    row = lambda v: v[None, :]
    out_lo, out_hi, grad_lo, grad_hi, g, t, s = mixer(
        S,
        (x_lo, x_hi, cot_lo, cot_hi, counts, wpack, column(b_tok2_lo), column(b_tok2_hi), w_chan_in, w_chan_out, row(b_chan_in), row(b_chan_out),
         row(ln1_gain), row(ln1_bias), row(ln2_gain), row(ln2_bias)),
    )
    g_in, g_out = widen(S, g)
    t = t.astype(f32).reshape(2, S.t_rows, 256)
    if groups is not None:
        g_in, g_out, t, s = lax.psum((g_in, g_out, t, s), "dp", axis_index_groups=groups)
    m = lax.axis_index("mp")
    ks = m * S.ks
    lo1 = lax.dynamic_slice(t[0], (S.t_lo + ks, 0), (S.ks, 256))[:, :S.p].T
    lo2 = lax.dynamic_slice(t[1], (S.t_lo + ks, 0), (S.ks, 256))[:, :S.p]
    n = S.own
    hi1 = jnp.concatenate([t[:, 0:n], t[:, 2 * n:3 * n, 0:128]], axis=2).reshape(2 * n, 384)
    hi2 = jnp.concatenate([t[:, n:2 * n], t[:, 2 * n:3 * n, 128:256]], axis=2).reshape(2 * n, 384)
    hi1 = lax.dynamic_slice(hi1, (0, ks), (S.ph, S.ks))
    hi2 = lax.dynamic_slice(hi2, (0, ks), (S.ph, S.ks)).T
    b2_hi = jnp.concatenate([s[12, :n], s[13, :n]])
    cut = lambda v, w: lax.dynamic_slice(v, (m * w,), (w,))
    return (
        out_lo, out_hi, grad_lo.astype(f32), grad_hi.astype(f32), s[3], s[4],
        lo1, cut(s[9], S.ks), lo2, cut(s[10], S.q), hi1, cut(s[11], S.ks), hi2, cut(b2_hi, S.qh),
        s[1], s[2], g_in, s[5:9].reshape(S.ff), g_out, s[0],
    )


def solution(mesh):
    blocks = mesh.shape["dp"] // (LINE * PAIR)
    groups = None
    if blocks > 1:
        size = LINE * PAIR
        groups = [[b * size + i for b in range(blocks)] for i in range(size)]
    tokens, rows = P("dp", "mp", None), P("dp", None)
    col, row, vec, rep = P(None, "mp"), P("mp", None), P("mp"), P()
    return jax.shard_map(
        functools.partial(body, groups),
        mesh=mesh,
        in_specs=(tokens,) * 4 + (rows, rep, rep) + (col, vec, row, vec) * 2 + (rep,) * 6,
        out_specs=(tokens,) * 4 + (rep, rep) + (col, vec, row, vec) * 2 + (rep,) * 6,
        check_vma=False,
    )
```

```python
import functools

import jax
import jax.numpy as jnp
from jax import lax
from jax.experimental import pallas as pl
from jax.experimental.pallas import tpu as pltpu
from jax.sharding import PartitionSpec as P

MESH = pl.DeviceIdType.MESH
EPS = 1e-06
GELU_A, GELU_B = 0.7978845608028654, 0.044715
f32, bf16 = jnp.float32, jnp.bfloat16

LINE, PAIR = 4, 2
SHARDS = 16
LAND = {"xzy": dict(x=0, z=8, y=18), "yzx": dict(y=0, z=8, x=18)}
LANDED = 19
CORE, X, Y, UP, DOWN, X_BACK, Y_BACK, UP_BACK, DOWN_BACK, CORE_BACK, NSEM = 0, 1, 2, 2, 5, 9, 10, 10, 13, 17, 18


class Place:
    def __init__(self):
        dp, mp = lax.axis_index("dp"), lax.axis_index("mp")
        self.block = dp // (LINE * PAIR)
        self.z = (dp // PAIR) % LINE
        self.x = dp % PAIR
        self.y = mp // 2
        self.c = mp % 2

    def at(self, z=None, x=None, y=None, c=None):
        z = self.z if z is None else z
        x = self.x if x is None else x
        y = self.y if y is None else y
        c = self.c if c is None else c
        return (self.block * (LINE * PAIR) + z * PAIR + x, y * 2 + c)

    def up(self):
        return self.at(z=jnp.minimum(self.z + 1, LINE - 1))

    def down(self):
        return self.at(z=jnp.maximum(self.z - 1, 0))

    def pair(self, axis):
        return self.at(**{axis: 1 - getattr(self, axis)})


def add_into(ref, idx, *others):
    total = ref[idx].astype(f32)
    for o in others:
        total = total + o.astype(f32)
    ref[idx] = total.astype(bf16)


class AllReduce:
    def __init__(self, place, g, land_core, land, out, send, recv, kept):
        self.p, self.g, self.lc, self.l, self.out, self.send, self.recv, self.kept = place, g, land_core, land, out, send, recv, kept
        self.unit = g.shape[1] // (2 * SHARDS)

    def sh(self, start, n):
        if isinstance(start, int):
            return pl.ds(start * self.unit, n * self.unit)
        return pl.ds(pl.multiple_of(start * self.unit, 16), n * self.unit)

    def copy(self, f, k, src, dst, dev):
        return pltpu.make_async_remote_copy(src, dst, self.send.at[f, k], self.recv.at[f, k], device_id=dev, device_id_type=MESH)

    def rows(self, start, n):
        return self.sh(self.p.c * SHARDS + start, n)

    def half(self, f, start, n):
        return self.g.at[f, self.rows(start, n)]

    def done(self, f, start, n):
        return self.out.at[f, self.rows(start, n)]

    def land(self, f, start, n):
        return self.l.at[f, self.sh(start, n)]

    def added(self, f, start, n, off):
        return lambda: add_into(self.g, (f, self.rows(start, n)), self.l[f, self.sh(off, n)])

    def core(self, f):
        p = self.p
        slot = f % self.lc.shape[0]
        src = self.g.at[f, self.sh((1 - p.c) * SHARDS, SHARDS)]
        return [(None, None, self.copy(f, CORE, src, self.lc.at[slot], p.pair("c")),
                 lambda: add_into(self.g, (f, self.rows(0, SHARDS)), self.lc[slot]))]

    def regions(self, path):
        base, n, out = 0, SHARDS, {}
        for axis in path:
            out[axis] = (base, n)
            n = n // (LINE if axis == "z" else PAIR)
            base = base + getattr(self.p, axis) * n
        out["end"] = (base, n)
        return out

    def pair(self, f, path, axis):
        base, n = self.regions(path)[axis]
        mine, off, m = getattr(self.p, axis), LAND[path][axis], n // 2
        k = {"x": X, "y": Y}[axis]
        return [(None, None, self.copy(f, k, self.half(f, base + (1 - mine) * m, m), self.land(f, off, m), self.p.pair(axis)),
                 self.added(f, base + mine * m, m, off))]

    def line(self, f, path, k):
        base, n = self.regions(path)["z"]
        z, m = self.p.z, n // LINE
        off = LAND[path]["z"]
        above, below = off + (LINE - 1 - k) * m, off + (1 + k) * m
        inside = lambda p: base + jnp.clip(p, 0, LINE - 1) * m
        up = self.copy(f, UP + k, self.half(f, inside(z + LINE - k), m), self.land(f, above, m), self.p.up())
        down = self.copy(f, DOWN + k, self.half(f, inside(z - LINE + k), m), self.land(f, below, m), self.p.down())
        return [((z < LINE - 1) & (z <= k - 1), (z > 0) & (z <= k), up, self.added(f, inside(z + LINE - 1 - k), m, above)),
                ((z > 0) & (z >= LINE - k), (z < LINE - 1) & (z >= LINE - 1 - k), down, self.added(f, inside(z - LINE + 1 + k), m, below))]

    def pair_back(self, f, path, axis):
        base, n = self.regions(path)[axis]
        at, m = base + getattr(self.p, axis) * (n // 2), n // 2
        k = {"x": X_BACK, "y": Y_BACK}[axis]
        ref = self.done(f, at, m)
        if axis == path[-1]:
            src = self.half(f, at, m)
            return [(None, None, self.copy(f, k, src, ref, self.p.pair(axis)), None),
                    (None, None, pltpu.make_async_copy(src, ref, self.kept.at[f]), None)]
        return [(None, None, self.copy(f, k, ref, ref, self.p.pair(axis)), None)]

    def line_back(self, f, path, k):
        base, n = self.regions(path)["z"]
        z, m = self.p.z, n // LINE
        inside = lambda p: self.done(f, base + jnp.clip(p, 0, LINE - 1) * m, m)
        up, down = inside(z + 1 - k), inside(z + k - 1)
        return [((z < LINE - 1) & (z >= k - 1), (z > 0) & (z >= k), self.copy(f, UP_BACK + k, up, up, self.p.up()), None),
                ((z > 0) & (z <= LINE - k), (z < LINE - 1) & (z <= LINE - 1 - k), self.copy(f, DOWN_BACK + k, down, down, self.p.down()), None)]

    def core_back(self, f):
        ref = self.done(f, 0, SHARDS)
        return [(None, None, self.copy(f, CORE_BACK, ref, ref, self.p.pair("c")), None)]

    def steps(self, path):
        seq = [self.core]
        for axis in path:
            if axis == "z":
                seq += [functools.partial(self.line, path=path, k=k) for k in range(1, LINE)]
            else:
                seq.append(functools.partial(self.pair, path=path, axis=axis))
        for axis in path[::-1]:
            if axis == "z":
                seq += [functools.partial(self.line_back, path=path, k=k) for k in range(1, LINE)]
            else:
                seq.append(functools.partial(self.pair_back, path=path, axis=axis))
        return seq + [self.core_back]

    def run_stage(self, f, s, path):
        seq = self.steps(path)
        if s > 0:
            for sends, gets, cp, then in seq[s - 1](f):
                if sends is None:
                    cp.wait()
                    if then is not None:
                        then()
                    continue
                pl.when(sends)(cp.wait_send)

                @pl.when(gets)
                def _():
                    cp.wait_recv()
                    if then is not None:
                        then()
        if s < len(seq):
            for sends, gets, cp, then in seq[s](f):
                if sends is None:
                    cp.start()
                else:
                    pl.when(sends)(cp.start)

    def step(self, i, last, paths, offsets):
        n = len(offsets)
        for s in range(n - 1, -1, -1):
            f = i - offsets[s]

            def go(f=f, s=s):
                if s in (0, n - 1):
                    self.run_stage(f, s, "xzy")
                    return
                for path, takes in paths(self.p.c, f):
                    @pl.when(takes)
                    def _():
                        self.run_stage(f, s, path)
            pl.when((f >= 0) & (f < last))(go)


STAGES = 2 * (2 + LINE) + 1


def paths(core, f):
    return [("xzy", core == 0), ("yzx", core == 1)]


OFFSETS = [0, 1] + [2 * s - 1 for s in range(2, STAGES - 1)] + [2 * STAGES - 4]
CORE_SLOTS = 4
T_OFFSETS = [0, 1, 3, 4, 6, 7, 9, 10, 12, 13, 15]
CHUNK = 256
SMALL = 16


def mm(a, b, ca=1, cb=0):
    return lax.dot_general(a, b, (((ca,), (cb,)), ((), ())), preferred_element_type=f32)


def gelu(v):
    return v * (0.5 * (1.0 + jnp.tanh(GELU_A * v * (1.0 + GELU_B * (v * v)))))


def gelu_both(v):
    sq = v * v
    t = jnp.tanh(GELU_A * v * (1.0 + GELU_B * sq))
    h = 0.5 * (1.0 + t)
    return v * h, h + 0.5 * v * (1.0 - t * t) * (GELU_A * (1.0 + 3.0 * GELU_B * sq))


def centred(v):
    c = v - jnp.mean(v, -1, keepdims=True)
    return c, lax.rsqrt(jnp.mean(c * c, -1, keepdims=True) + EPS)


def norm_back(c, rs, u):
    xh = c * rs
    return (u - jnp.mean(u, -1, keepdims=True) - xh * jnp.mean(u * xh, -1, keepdims=True)) * rs


def colsum(v):
    return jnp.sum(v, 0, keepdims=True)


def up16(n):
    return -(-n // 16) * 16


def up128(n):
    return -(-n // 128) * 128


class Sizes:
    def __init__(self, x_lo, x_hi, w_tok1_lo, w_chan_in):
        self.slots, self.q, self.d = x_lo.shape
        self.imgs = self.slots // 4
        self.qh = x_hi.shape[1]
        self.p, self.ph = 4 * self.q, 4 * self.qh
        self.ks = w_tok1_lo.shape[0]
        self.k = 4 * self.ks
        self.ff = w_chan_in.shape[1]
        self.chunks = self.ff // CHUNK
        self.pr = up16(self.p)
        self.own = 2 * self.qh
        self.hi0 = self.imgs * self.pr
        self.rows = self.hi0 + self.own
        self.half_rows = CHUNK * (self.d // 256)
        self.hb = -(-self.ph // 256)
        self.blocks = 2 + 2 * self.hb


def kernel(
    S,
    x_lo, x_hi, cot_lo, cot_hi, counts, w1l, b1l, w2l, b2l, w1h, b1h, w2h, b2h, w_in, w_out, b_in, b_out, gain1, shift1, gain2, shift2,
    out_lo, out_hi, grad_lo, grad_hi, g_sum, t_sum, s_sum,
    xl, xh, cl, ch, wg, bl, bho, bh, w2t_lo, w1_lo, w2t_hi, w1_hi, bcol, bcols, brow, af, nb, nh, n2, ct, tmp, gmh, hid, gp, winv, woutv,
    g, g_core, g_land, t, t_core, t_land, gw1, gw2, gb, sv, s1, s2,
    lo_send, lo_recv, hi_send, hi_recv, w_send, w_recv, ring_send, ring_recv, g_send, g_recv, t_send, t_recv,
    s_send, s_recv, local, g_kept, t_kept,
):
    p = Place()
    y, c = p.y, p.c
    m = y * 2 + c
    dpi = p.z * PAIR + p.x
    peers = [(y, 1 - c), (1 - y, c), (1 - y, 1 - c)]
    d = S.d

    def dev(yy, cc):
        return p.at(y=yy, c=cc)

    def rcopy(src, dst, send, recv, to):
        return pltpu.make_async_remote_copy(src, dst, send, recv, device_id=to, device_id_type=MESH)

    def dp_dev(k):
        i = (dpi + k) % (LINE * PAIR)
        return p.at(z=i // PAIR, x=i % PAIR)

    sem = pltpu.get_barrier_semaphore()
    for yy, cc in peers:
        pl.semaphore_signal(sem, inc=1, device_id=dev(yy, cc), device_id_type=MESH)
    for k in range(1, LINE * PAIR):
        pl.semaphore_signal(sem, inc=1, device_id=dp_dev(k), device_id_type=MESH)
    pl.semaphore_wait(sem, 3 + LINE * PAIR - 1)

    def lo_out(kind, i, src, dst):
        res = []
        for j, (yy, cc) in enumerate(peers):
            mm_ = yy * 2 + cc
            res.append(rcopy(src.at[S.imgs * mm_ + i], dst.at[m, i], lo_send.at[kind, j, i], lo_recv.at[kind, m, i], dev(yy, cc)))
        return res

    def lo_in(kind, i, dst):
        return [rcopy(dst.at[yy * 2 + cc, i], dst.at[yy * 2 + cc, i], lo_send.at[kind, j, i], lo_recv.at[kind, yy * 2 + cc, i], dev(yy, cc)) for j, (yy, cc) in enumerate(peers)]

    def lo_local(kind, i, src, dst):
        return pltpu.make_async_copy(src.at[S.imgs * m + i], dst.at[m, i], local.at[kind, i])

    def lo_back(kind, i, src, dst):
        return [rcopy(src.at[yy * 2 + cc, i], dst.at[S.imgs * m + i], lo_send.at[kind, j, i], lo_recv.at[kind, m, i], dev(yy, cc)) for j, (yy, cc) in enumerate(peers)]

    def lo_back_in(kind, i, dst):
        return [rcopy(dst.at[S.imgs * (yy * 2 + cc) + i], dst.at[S.imgs * (yy * 2 + cc) + i], lo_send.at[kind, j, i], lo_recv.at[kind, yy * 2 + cc, i], dev(yy, cc)) for j, (yy, cc) in enumerate(peers)]

    def lo_back_local(kind, i, src, dst):
        return pltpu.make_async_copy(src.at[m, i], dst.at[S.imgs * m + i], local.at[kind, i])

    def hi_out(kind, src, dst):
        res = []
        for h in range(2):
            mine = (y == h) & (c == y)
            ref = src.at[h] if src.shape[0] == 2 and len(src.shape) == 3 else src
            res.append((mine, rcopy(ref, dst.at[c], hi_send.at[kind, h], hi_recv.at[kind, c], dev(h, y)),
                        pltpu.make_async_copy(ref, dst.at[c], local.at[kind, S.imgs])))
        return res

    def hi_in(kind, dst):
        res = []
        for j in range(2):
            mine = (y == c) & (c == j)
            res.append((mine, rcopy(dst.at[j], dst.at[j], hi_send.at[kind, j], hi_recv.at[kind, j], dev(c, j))))
        return res

    def hi_back(kind, src, dst):
        res = []
        for j in range(2):
            mine = (y == c) & (c == j)
            res.append((mine, rcopy(src.at[j], dst.at[y], hi_send.at[kind, j], hi_recv.at[kind, y], dev(c, j)),
                        pltpu.make_async_copy(src.at[j], dst.at[y], local.at[kind, S.imgs])))
        return res

    def hi_back_in(kind, dst):
        res = []
        for h in range(2):
            mine = (y == h) & (c == y)
            res.append((mine, rcopy(dst.at[h], dst.at[h], hi_send.at[kind, h], hi_recv.at[kind, h], dev(h, y))))
        return res

    def start(copies):
        for cp in copies:
            cp.start()

    def start_hi(copies):
        for mine, remote, here in copies:
            pl.when(mine)(here.start)
            pl.when(jnp.logical_not(mine))(remote.start)

    def sent_hi(copies):
        for mine, remote, here in copies:
            pl.when(mine)(here.wait)
            pl.when(jnp.logical_not(mine))(remote.wait_send)

    def got_hi(copies):
        for mine, remote in copies:
            pl.when(jnp.logical_not(mine))(remote.wait_recv)

    my = (1 - y) * 2 + c

    def across(v, lanes):
        n = v.shape[0]
        return jnp.broadcast_to(v[...].astype(f32).reshape(1, n), (lanes, n)).T.astype(bf16)

    start_hi(hi_out(0, x_hi, xh))
    wg[m] = jnp.zeros((S.blocks, S.ks, 256), bf16)
    wg[m, 0, :, 128:256] = across(b1l, 128)
    wg[m, 1 + S.hb, :, 128:256] = across(b1h, 128)
    wg[m, 0, :, 0:S.pr] = jnp.zeros((S.ks, S.pr), bf16)
    wg[m, 0, :, 0:S.p] = w1l[...]
    wg[m, 1, :, 0:S.p] = w2l[...]
    for j in range(S.hb):
        n = min(256, S.ph - 256 * j)
        wg[m, 2 + j, :, 0:n] = w1h[:, 256 * j:256 * j + n]
        wg[m, 2 + S.hb + j, :, 0:n] = w2h[:, 256 * j:256 * j + n]
    w_y = rcopy(wg.at[m, dpi], wg.at[m, dpi], w_send.at[0], w_recv.at[0], dev(1 - y, c))
    w_y_in = rcopy(wg.at[my, dpi], wg.at[my, dpi], w_send.at[0], w_recv.at[0], dev(1 - y, c))
    w_c = rcopy(wg.at[m], wg.at[m], w_send.at[1], w_recv.at[1], dev(y, 1 - c))
    w_f = rcopy(wg.at[my], wg.at[my], w_send.at[2], w_recv.at[2], dev(y, 1 - c))
    w_d = [rcopy(wg.at[my, dpi], wg.at[my, dpi], w_send.at[6 + k], w_recv.at[7 + dpi], dp_dev(k)) for k in range(1, LINE * PAIR)]
    w_y.start()
    w_c.start()
    bl[m] = across(b2l, 128)
    bias_out = [rcopy(bl.at[m], bl.at[m], w_send.at[3 + j], w_recv.at[3 + m], dev(yy, cc)) for j, (yy, cc) in enumerate(peers)]
    start(bias_out)
    bho[...] = across(b2h, 128)
    bias_hi_out = hi_out(4, bho, bh)
    start_hi(bias_hi_out)
    for i in range(S.imgs):
        start(lo_out(0, i, x_lo, xl))
        lo_local(0, i, x_lo, xl).start()
    start_hi(hi_out(1, cot_hi, ch))
    for i in range(S.imgs):
        start(lo_out(1, i, cot_lo, cl))
        lo_local(1, i, cot_lo, cl).start()
    load_in = pltpu.make_async_copy(w_in, winv, local.at[4, 1])
    load_out = pltpu.make_async_copy(w_out, woutv, local.at[4, 2])
    load_in.start()
    load_out.start()

    def line_of(v):
        return v[...].astype(f32).reshape(1, v.shape[0])

    gv1, sv1 = line_of(gain1), line_of(shift1)
    gv2, sv2 = line_of(gain2), line_of(shift2)
    brow[...] = line_of(b_in)
    hi = pl.ds(S.hi0, S.own)
    own = pl.ds(pl.multiple_of(c * S.own, 16), S.own)

    def img(i):
        return pl.ds(pl.multiple_of(i * S.pr, 16), S.pr)

    def gather_rows(block, i):
        for s in range(4):
            tmp[s * S.q:(s + 1) * S.q, :] = block[s, i].astype(f32)
        if S.pr > S.p:
            tmp[S.p:S.pr, :] = jnp.zeros((S.pr - S.p, d), f32)

    def scatter_rows(block, i):
        for s in range(4):
            block[s, i] = tmp[s * S.q:(s + 1) * S.q, :].astype(bf16)

    sv[...] = jnp.zeros_like(sv)
    t[...] = jnp.zeros_like(t)
    gw1[...] = jnp.zeros_like(gw1)
    gw2[...] = jnp.zeros_like(gw2)

    got_hi(hi_in(0, xh))
    sent_hi(hi_out(0, x_hi, xh))
    v = xh[...].reshape(S.own, d).astype(f32)
    cen, rs = centred(v)
    n = (cen * rs * gv1 + sv1).astype(bf16)
    nb[hi, :] = n
    nh[own, :] = n
    af[hi, :] = v
    nh_copy = rcopy(nh.at[own], nh.at[own], ring_send.at[0], ring_recv.at[0], dev(y, 1 - c))
    nh_copy.start()

    w_y.wait_send()
    w_y_in.wait_recv()
    start(w_d)
    for k in range(1, LINE * PAIR):
        i = (dpi + k) % (LINE * PAIR)
        w_d[k - 1].wait_send()
        rcopy(wg.at[my, i], wg.at[my, i], w_send.at[6 + k], w_recv.at[7 + i], dp_dev(k)).wait_recv()
    w_f.start()
    w_c.wait()
    w_f.wait_send()
    w_far = rcopy(wg.at[(1 - y) * 2 + 1 - c], wg.at[(1 - y) * 2 + 1 - c], w_send.at[2], w_recv.at[2], dev(y, 1 - c))
    w_far.wait_recv()

    def block(b, n):
        return wg[:, b, :, 0:n].reshape(S.k, n)

    def w1t_lo():
        return block(0, S.pr)

    def w2_lo():
        return block(1, S.pr)

    def bias_of(b):
        return wg[:, b, :, 128:256].reshape(S.k, 128).astype(f32)[:, 127:128]

    spans = [(256 * j, min(256, S.ph - 256 * j)) for j in range(S.hb)]

    def mm_hi(first, rows_of):
        return functools.reduce(jnp.add, [mm(block(first + j, n), rows_of[at:at + n, :]) for j, (at, n) in enumerate(spans)])

    for k in range(2):
        bcols[k] = jnp.broadcast_to(bias_of(k * (1 + S.hb)), (S.k, 128))

    def b1_lo():
        return bcols[0, :, 0:1]

    def b1_hi():
        return bcols[1, :, 0:1]

    w1_lo[...] = w1t_lo().T
    w2t_lo[...] = w2_lo().T
    for j, (at, n) in enumerate(spans):
        w1_hi[at:at + n, :] = block(2 + j, n).T
        w2t_hi[at:at + n, :] = block(2 + S.hb + j, n).T
    for j, (yy, cc) in enumerate(peers):
        bias_out[j].wait_send()
        s = yy * 2 + cc
        rcopy(bl.at[s], bl.at[s], w_send.at[3 + j], w_recv.at[3 + s], dev(yy, cc)).wait_recv()
    got_hi(hi_in(4, bh))
    sent_hi(bias_hi_out)
    bcol[...] = jnp.zeros_like(bcol)
    for s in range(4):
        bcol[s * S.q:(s + 1) * S.q, :] = bl[s].astype(f32)

    def fwd_lo(i, carry):
        for cp in lo_in(0, i, xl):
            cp.wait_recv()
        lo_local(0, i, x_lo, xl).wait()
        gather_rows(xl, i)
        v = tmp[...]
        cen, rs = centred(v)
        n = (cen * rs * gv1 + sv1).astype(bf16)
        nb[img(i), :] = n
        ht = gelu(mm(w1t_lo(), n) + b1_lo()).astype(bf16)
        af[img(i), :] = v + (mm(w2t_lo[...], ht) + bcol[:, 0:1])
        return carry

    lax.fori_loop(0, S.imgs, fwd_lo, 0)
    nh_copy.wait()
    ht = gelu(mm_hi(2, nh) + b1_hi()).astype(bf16)
    bcol_hi = bh[...].reshape(S.own, 128).astype(f32)[:, 0:1]
    af[hi, :] = af[hi, :] + (mm(w2t_hi[own, :], ht) + bcol_hi)

    def norm_two(rows):
        cen, rs = centred(af[rows, :])
        n2[rows, :] = (cen * rs * gv2 + sv2).astype(bf16)

    norm_two(hi)

    def norm_lo(i, carry):
        norm_two(img(i))
        return carry

    lax.fori_loop(0, S.imgs, norm_lo, 0)

    def live_lo(i):
        return jnp.where(S.imgs * m + i < counts[0, 0], 1.0, 0.0).astype(f32)

    live_hi = jnp.where(y < counts[0, 1], 1.0, 0.0).astype(f32)
    got_hi(hi_in(1, ch))
    sent_hi(hi_out(1, cot_hi, ch))
    ct[hi, :] = (ch[...].reshape(S.own, d).astype(f32) * live_hi).astype(bf16)

    def cot_rows(i, carry):
        for cp in lo_in(1, i, cl):
            cp.wait_recv()
        lo_local(1, i, cot_lo, cl).wait()
        gather_rows(cl, i)
        ct[img(i), :] = (tmp[...] * live_lo(i)).astype(bf16)
        return carry

    lax.fori_loop(0, S.imgs, cot_rows, 0)
    for kind, src, dst in ((0, x_lo, xl), (1, cot_lo, cl)):
        for i in range(S.imgs):
            for cp in lo_out(kind, i, src, dst):
                cp.wait_send()
    load_in.wait()
    load_out.wait()

    def channel(f):
        cols = pl.ds(pl.multiple_of(f * CHUNK, CHUNK), CHUNK)
        h, slope = gelu_both(mm(n2[...], winv[:, cols]) + brow[:, cols])
        hb = h.astype(bf16)
        hid[:, cols] = hb
        gpre = (mm(ct[...], woutv[cols, :], 1, 1) * slope).astype(bf16)
        gp[:, cols] = gpre
        gb[:, cols] = colsum(gpre.astype(f32))
        g[f, 0:d, :] = mm(n2[...], gpre, 0, 0).astype(bf16)
        grad = mm(hb, ct[...], 0, 0)
        for j in range(d // 256):
            g[f, S.half_rows + CHUNK * j:S.half_rows + CHUNK * (j + 1), :] = grad[:, 256 * j:256 * (j + 1)].astype(bf16)

    bo = line_of(b_out)

    def channel_back(rows, live):
        a = af[rows, :]
        out = (a + mm(hid[rows, :], woutv[...]) + bo) * live
        gn = mm(gp[rows, :], winv[...], 1, 1)
        cen, rs = centred(a)
        c_rows = ct[rows, :].astype(f32)
        grad = c_rows + norm_back(cen, rs, gn * gv2)
        sv[0:1, :] += colsum(c_rows)
        sv[1:2, :] += colsum(gn * (cen * rs))
        sv[2:3, :] += colsum(gn)
        af[rows, :] = grad
        n2[rows, :] = grad.astype(bf16)
        return out

    def back_hi():
        out = channel_back(hi, live_hi)
        ch[...] = out.astype(bf16).reshape(2, S.qh, d)
        start_hi(hi_back(2, ch, out_hi))
        gmh[own, :] = n2[hi, :]
        gm_copy.start()

    gm_copy = rcopy(gmh.at[own], gmh.at[own], ring_send.at[1], ring_recv.at[1], dev(y, 1 - c))

    def back_lo(i):
        tmp[...] = channel_back(img(i), live_lo(i))
        scatter_rows(cl, i)
        start(lo_back(2, i, cl, out_lo))
        lo_back_local(2, i, cl, out_lo).start()

    ones = jnp.ones((8, d), bf16)

    def first_norm_back(v, gn, rows):
        cen, rs = centred(v)
        sv[3:4, :] += colsum(gn * (cen * rs))
        sv[4:5, :] += colsum(gn)
        return af[rows, :] + norm_back(cen, rs, gn * gv1)

    def token_lo(i):
        n = nb[img(i), :]
        gm = n2[img(i), :]
        h, slope = gelu_both(mm(w1t_lo(), n) + b1_lo())
        gw2[:, 0:S.pr] += mm(h.astype(bf16), gm, 1, 1)
        gpt = (mm(w2_lo(), gm) * slope).astype(bf16)
        gw1[:, 0:S.pr] += mm(gpt, n, 1, 1)
        sv[9:10, 0:S.k] += mm(ones, gpt, 1, 1)[0:1]
        sv[10:11, 0:S.pr] += mm(ones, gm, 1, 1)[0:1]
        gn = mm(w1_lo[...], gpt)
        gather_rows(xl, i)
        tmp[...] = first_norm_back(tmp[...], gn, img(i))
        scatter_rows(xl, i)
        start(lo_back(3, i, xl, grad_lo))
        lo_back_local(3, i, xl, grad_lo).start()

    def token_hi():
        gm_copy.wait()
        n = nb[hi, :]
        gm = n2[hi, :]
        h, slope = gelu_both(mm_hi(2, nh) + b1_hi())
        ga2 = mm(h.astype(bf16), gmh[...], 1, 1) * 0.5
        gpt = (mm_hi(2 + S.hb, gmh) * slope).astype(bf16)
        ga1 = mm(gpt, nh[...], 1, 1) * 0.5
        sv[11:12, 0:S.k] += mm(ones, gpt, 1, 1)[0:1] * 0.5
        sv[pl.ds(12 + c, 1), 0:S.own] = mm(ones, gm, 1, 1)[0:1]
        gn = mm(w1_hi[own, :], gpt)
        grad = first_norm_back(xh[...].reshape(S.own, d).astype(f32), gn, hi)
        xh[...] = grad.astype(bf16).reshape(2, S.qh, d)
        start_hi(hi_back(3, xh, grad_hi))
        for j in range(S.ff // d):
            sv[5 + j:6 + j, :] = gb[:, d * j:d * (j + 1)]
        s1[m] = sv[...]
        start(s1_out)
        for ks in range(4):
            k0, yy, cc = ks * S.ks, ks // 2, ks % 2

            def put(j, v, n=256):
                row = (cc * SHARDS + 2 * j + yy) * S.ks
                t[0, row:row + S.ks, 0:n] = v.astype(bf16)

            put(0, gw1[k0:k0 + S.ks, :])
            put(1, gw2[k0:k0 + S.ks, :])
            for j in range(S.hb):
                n = min(256, S.ph - 256 * j)
                put(2 + j, ga1[k0:k0 + S.ks, 256 * j:256 * j + n], n)
                put(2 + S.hb + j, ga2[k0:k0 + S.ks, 256 * j:256 * j + n], n)

    s1_out = [rcopy(s1.at[m], s1.at[m], s_send.at[j], s_recv.at[m], dev(yy, cc)) for j, (yy, cc) in enumerate(peers)]
    s2_out = [rcopy(s2.at[dpi], s2.at[dpi], s_send.at[3 + k], s_recv.at[4 + dpi], dp_dev(k)) for k in range(1, LINE * PAIR)]

    ar = AllReduce(p, g, g_core, g_land, g_sum, g_send, g_recv, g_kept)
    art = TokenSum(p, t, t_core, t_land, t_sum, t_send, t_recv, t_kept)
    nc = S.chunks
    b0 = nc + 1 + S.imgs
    t0 = b0 + S.imgs

    def step(i, carry):
        pl.when(i < nc)(lambda: channel(i))
        pl.when(i == nc)(back_hi)
        pl.when((i > nc) & (i < b0))(lambda: back_lo(i - nc - 1))
        pl.when((i >= b0) & (i < t0))(lambda: token_lo(i - b0))
        pl.when(i == t0)(token_hi)
        pl.when(i == t0 + 2)(small_sums)
        ar.step(i, nc, paths, OFFSETS)
        art.step(i - t0, T_OFFSETS)
        return carry

    def small_sums():
        for j, (yy, cc) in enumerate(peers):
            s = yy * 2 + cc
            s1_out[j].wait_send()
            rcopy(s1.at[s], s1.at[s], s_send.at[j], s_recv.at[s], dev(yy, cc)).wait_recv()
        s2[dpi] = s1[0] + s1[1] + s1[2] + s1[3]
        start(s2_out)

    lax.fori_loop(0, max(nc + OFFSETS[-1], t0 + 1 + T_OFFSETS[-1]), step, 0)
    for k in range(1, LINE * PAIR):
        i = (dpi + k) % (LINE * PAIR)
        s2_out[k - 1].wait_send()
        rcopy(s2.at[i], s2.at[i], s_send.at[3 + k], s_recv.at[4 + i], dp_dev(k)).wait_recv()
    total = s2[0]
    for i in range(1, LINE * PAIR):
        total = total + s2[i]
    s_sum[...] = total

    for kind, src, src_hi, dst, dst_hi in ((2, cl, ch, out_lo, out_hi), (3, xl, xh, grad_lo, grad_hi)):
        for i in range(S.imgs):
            for cp in lo_back(kind, i, src, dst):
                cp.wait_send()
            for cp in lo_back_in(kind, i, dst):
                cp.wait_recv()
            lo_back_local(kind, i, src, dst).wait()
        sent_hi(hi_back(kind, src_hi, dst_hi))
        got_hi(hi_back_in(kind, dst_hi))


def mixer(S, args):
    V = pl.BlockSpec(memory_space=pltpu.VMEM)
    A = pl.BlockSpec(memory_space=pl.ANY)
    M = pl.BlockSpec(memory_space=pltpu.SMEM)
    sds = jax.ShapeDtypeStruct
    d, dma = S.d, pltpu.SemaphoreType.DMA
    nc = S.chunks
    unit = 2 * S.half_rows // (2 * SHARDS)
    scratch = [
        pltpu.VMEM((4, S.imgs, S.q, d), bf16), pltpu.VMEM((2, S.qh, d), bf16),
        pltpu.VMEM((4, S.imgs, S.q, d), bf16), pltpu.VMEM((2, S.qh, d), bf16),
        pltpu.VMEM((4, S.blocks, S.ks, 256), bf16), pltpu.VMEM((4, S.q, 128), bf16), pltpu.VMEM((S.qh, 128), bf16), pltpu.VMEM((2, S.qh, 128), bf16),
        pltpu.VMEM((S.pr, S.k), bf16), pltpu.VMEM((S.pr, S.k), bf16), pltpu.VMEM((S.ph, S.k), bf16), pltpu.VMEM((S.ph, S.k), bf16),
        pltpu.VMEM((S.pr, 128), f32), pltpu.VMEM((2, S.k, 128), f32), pltpu.VMEM((1, S.ff), f32),
        pltpu.VMEM((S.rows, d), f32), pltpu.VMEM((S.rows, d), bf16), pltpu.VMEM((S.ph, d), bf16), pltpu.VMEM((S.rows, d), bf16),
        pltpu.VMEM((S.rows, d), bf16), pltpu.VMEM((S.pr, d), f32), pltpu.VMEM((S.ph, d), bf16),
        pltpu.VMEM((S.rows, S.ff), bf16), pltpu.VMEM((S.rows, S.ff), bf16), pltpu.VMEM((d, S.ff), bf16), pltpu.VMEM((S.ff, d), bf16),
        pltpu.VMEM((nc, 2 * SHARDS * unit, 256), bf16), pltpu.VMEM((CORE_SLOTS, SHARDS * unit, 256), bf16), pltpu.VMEM((nc, LANDED * unit, 256), bf16),
        pltpu.VMEM((1, 2 * SHARDS * S.ks, 256), bf16), pltpu.VMEM((1, SHARDS * S.ks, 256), bf16), pltpu.VMEM((1, LANDED * S.ks, 256), bf16),
        pltpu.VMEM((S.k, 256), f32), pltpu.VMEM((S.k, 256), f32), pltpu.VMEM((1, S.ff), f32),
        pltpu.VMEM((SMALL, d), f32), pltpu.VMEM((4, SMALL, d), f32), pltpu.VMEM((LINE * PAIR, SMALL, d), f32),
        dma((4, 3, S.imgs)), dma((4, 4, S.imgs)), dma((5, 2)), dma((5, 2)), dma((14,)), dma((15,)), dma((2,)), dma((2,)),
        dma((nc, NSEM)), dma((nc, NSEM)), dma((1, NSEM)), dma((1, NSEM)), dma((11,)), dma((12,)), dma((5, S.imgs + 1)), dma((nc,)), dma((1,)),
    ]
    return pl.pallas_call(
        functools.partial(kernel, S),
        out_shape=(
            sds((S.slots, S.q, d), bf16), sds((2, S.qh, d), bf16), sds((S.slots, S.q, d), bf16), sds((2, S.qh, d), bf16),
            sds((nc, 2 * S.half_rows, 256), bf16), sds((1, S.blocks * S.ks, 256), bf16), sds((SMALL, d), f32),
        ),
        in_specs=[A, A, A, A, M] + [V] * 8 + [A, A] + [V] * 6,
        out_specs=(A, A, A, A, A, A, V),
        scratch_shapes=scratch,
        compiler_params=pltpu.CompilerParams(collective_id=0, has_side_effects=True, vmem_limit_bytes=63 * 1024 * 1024),
    )(*args)


class TokenSum(AllReduce):
    def part(self, i):
        return self.out.at[0, self.sh(i, 1)]

    def line_back(self, f, path, k):
        z, base = self.p.z, self.p.x * LINE
        inside = lambda p: self.part(base + jnp.clip(p, 0, LINE - 1))
        up, down = inside(z + 1 - k), inside(z + k - 1)
        up_src, down_src, more = up, down, []
        if k == 1:
            up_src = down_src = self.half(f, (base + z) * PAIR + self.p.y, 1)
            more = [(None, None, pltpu.make_async_copy(up_src, up, self.kept.at[f]), None)]
        return [((z < LINE - 1) & (z >= k - 1), (z > 0) & (z >= k), self.copy(f, UP_BACK + k, up_src, up, self.p.up()), None),
                ((z > 0) & (z <= LINE - k), (z < LINE - 1) & (z <= LINE - 1 - k), self.copy(f, DOWN_BACK + k, down_src, down, self.p.down()), None)] + more

    def x_back(self, f):
        ref = self.out.at[0, self.sh(self.p.x * LINE, LINE)]
        return [(None, None, self.copy(f, X_BACK, ref, ref, self.p.pair("x")), None)]

    def steps(self, path):
        there = super().steps(path)[:2 + LINE]
        return there + [functools.partial(self.line_back, path=path, k=k) for k in range(1, LINE)] + [self.x_back]

    def step(self, i, offsets):
        for s in range(len(offsets)):
            pl.when(i == offsets[s])(functools.partial(self.run_stage, 0, s, "xzy"))


def finish(S, out_lo, out_hi, grad_lo, grad_hi, g, t, s):
    d = S.d
    sds = jax.ShapeDtypeStruct

    def place(ol, oh, gl, gh, g_ref, t_ref, s_ref, *outs):
        (o_lo, o_hi, r_lo, r_hi, l1g, l1b, w1l, b1l, w2l, b2l, w1h, b1h, w2h, b2h, l2g, l2b, w_in, b_in, w_out, b_out) = outs
        m = lax.axis_index("mp")
        w_in[...] = g_ref[0, 0:d, :].astype(f32)
        for j in range(d // 256):
            w_out[:, 256 * j:256 * (j + 1)] = g_ref[0, S.half_rows + CHUNK * j:S.half_rows + CHUNK * (j + 1), :].astype(f32)
        o_lo[...] = ol[...]
        r_lo[...] = gl[...].astype(f32)

        @pl.when(pl.program_id(0) == 0)
        def _():
            o_hi[...] = oh[...]
            r_hi[...] = gh[...].astype(f32)
            w1l[...] = t_ref[0, :, 0:S.p].astype(f32)
            w2l[...] = t_ref[1, :, 0:S.p].astype(f32)
            for j in range(S.hb):
                n = min(256, S.ph - 256 * j)
                w1h[:, 256 * j:256 * j + n] = t_ref[2 + j, :, 0:n].astype(f32)
                w2h[:, 256 * j:256 * j + n] = t_ref[2 + S.hb + j, :, 0:n].astype(f32)
            for i, o in ((0, b_out), (1, l2g), (2, l2b), (3, l1g), (4, l1b)):
                o[...] = s_ref[i, :]
            for j in range(S.ff // d):
                b_in[d * j:d * (j + 1)] = s_ref[5 + j, :]
            for j in range(4):
                @pl.when(m == j)
                def _():
                    b1l[...] = s_ref[9, S.ks * j:S.ks * (j + 1)]
                    b2l[...] = s_ref[10, S.q * j:S.q * (j + 1)]
                    b1h[...] = s_ref[11, S.ks * j:S.ks * (j + 1)]
                    b2h[...] = s_ref[12 + j // 2, S.qh * (j % 2):S.qh * (j % 2 + 1)]

    def whole(v):
        return pl.BlockSpec(v.shape, lambda i: (0,) * len(v.shape))

    image = pl.BlockSpec((S.slots // S.chunks, S.q, d), lambda i: (i, 0, 0))
    vec = lambda n: sds((n,), f32)
    shapes = [
        sds(out_lo.shape, bf16), sds(out_hi.shape, bf16), sds(out_lo.shape, f32), sds(out_hi.shape, f32), vec(d), vec(d),
        sds((S.ks, S.p), f32), vec(S.ks), sds((S.ks, S.p), f32), vec(S.q), sds((S.ks, S.ph), f32), vec(S.ks), sds((S.ks, S.ph), f32), vec(S.qh),
        vec(d), vec(d), sds((d, S.ff), f32), vec(S.ff), sds((S.ff, d), f32), vec(d),
    ]
    outs = [whole(v) for v in shapes]
    outs[0] = outs[2] = image
    outs[16] = pl.BlockSpec((d, CHUNK), lambda i: (0, i))
    outs[18] = pl.BlockSpec((CHUNK, d), lambda i: (i, 0))
    t = t.reshape(S.blocks, S.ks, 256)
    return pl.pallas_call(
        place,
        grid=(S.chunks,),
        out_shape=shapes,
        in_specs=[image, whole(out_hi), image, whole(grad_hi), pl.BlockSpec((1, 2 * S.half_rows, 256), lambda i: (i, 0, 0)), whole(t), whole(s)],
        out_specs=outs,
        compiler_params=pltpu.CompilerParams(vmem_limit_bytes=63 * 1024 * 1024),
    )(out_lo, out_hi, grad_lo, grad_hi, g, t, s)


def body(
    groups,
    x_lo, x_hi, cot_lo, cot_hi, counts, ln1_gain, ln1_bias, w_tok1_lo, b_tok1_lo, w_tok2_lo, b_tok2_lo, w_tok1_hi, b_tok1_hi,
    w_tok2_hi, b_tok2_hi, ln2_gain, ln2_bias, w_chan_in, b_chan_in, w_chan_out, b_chan_out,
):
    w1_lo, w1_hi = w_tok1_lo.T, w_tok1_hi.T
    S = Sizes(x_lo, x_hi, w1_lo, w_chan_in)
    out_lo, out_hi, grad_lo, grad_hi, g, t, s = mixer(
        S,
        (x_lo, x_hi, cot_lo, cot_hi, counts, w1_lo, b_tok1_lo, w_tok2_lo, b_tok2_lo, w1_hi, b_tok1_hi, w_tok2_hi, b_tok2_hi,
         w_chan_in, w_chan_out, b_chan_in, b_chan_out, ln1_gain, ln1_bias, ln2_gain, ln2_bias),
    )
    if groups is not None:
        g, t, s = lax.psum((g.astype(f32), t.astype(f32), s), "dp", axis_index_groups=groups)
    res = list(finish(S, out_lo, out_hi, grad_lo, grad_hi, g, t, s))
    res[6], res[10] = res[6].T, res[10].T
    return tuple(res)


def solution(mesh):
    blocks = mesh.shape["dp"] // (LINE * PAIR)
    groups = None
    if blocks > 1:
        size = LINE * PAIR
        groups = [[b * size + i for b in range(blocks)] for i in range(size)]
    tokens, rows = P("dp", "mp", None), P("dp", None)
    col, row, vec, rep = P(None, "mp"), P("mp", None), P("mp"), P()
    return jax.shard_map(
        functools.partial(body, groups),
        mesh=mesh,
        in_specs=(tokens,) * 4 + (rows, rep, rep) + (col, vec, row, vec) * 2 + (rep,) * 6,
        out_specs=(tokens,) * 4 + (rep, rep) + (col, vec, row, vec) * 2 + (rep,) * 6,
        check_vma=False,
    )
```

```python
import functools

import jax
import jax.numpy as jnp
from jax import lax
from jax.experimental import pallas as pl
from jax.experimental.pallas import tpu as pltpu
from jax.sharding import PartitionSpec as P

MESH = pl.DeviceIdType.MESH
EPS = 1e-06
GELU_A, GELU_B = 0.7978845608028654, 0.044715
f32, bf16 = jnp.float32, jnp.bfloat16

LINE, PAIR = 4, 2
SHARDS = 16
LAND = {"xzy": dict(x=0, z=8, y=18), "yzx": dict(y=0, z=8, x=18)}
LANDED = 19
CORE, X, Y, UP, DOWN, X_BACK, Y_BACK, UP_BACK, DOWN_BACK, CORE_BACK, NSEM = 0, 1, 2, 2, 5, 9, 10, 10, 13, 17, 18


class Place:
    def __init__(self):
        dp, mp = lax.axis_index("dp"), lax.axis_index("mp")
        self.block = dp // (LINE * PAIR)
        self.z = (dp // PAIR) % LINE
        self.x = dp % PAIR
        self.y = mp // 2
        self.c = mp % 2

    def at(self, z=None, x=None, y=None, c=None):
        z = self.z if z is None else z
        x = self.x if x is None else x
        y = self.y if y is None else y
        c = self.c if c is None else c
        return (self.block * (LINE * PAIR) + z * PAIR + x, y * 2 + c)

    def up(self):
        return self.at(z=jnp.minimum(self.z + 1, LINE - 1))

    def down(self):
        return self.at(z=jnp.maximum(self.z - 1, 0))

    def pair(self, axis):
        return self.at(**{axis: 1 - getattr(self, axis)})


def add_into(ref, idx, *others):
    total = ref[idx].astype(f32)
    for o in others:
        total = total + o.astype(f32)
    ref[idx] = total.astype(bf16)


class AllReduce:
    def __init__(self, place, g, land_core, land, out, send, recv, kept):
        self.p, self.g, self.lc, self.l, self.out, self.send, self.recv, self.kept = place, g, land_core, land, out, send, recv, kept
        self.unit = g.shape[1] // (2 * SHARDS)

    def sh(self, start, n):
        if isinstance(start, int):
            return pl.ds(start * self.unit, n * self.unit)
        return pl.ds(pl.multiple_of(start * self.unit, 16), n * self.unit)

    def copy(self, f, k, src, dst, dev):
        return pltpu.make_async_remote_copy(src, dst, self.send.at[f, k], self.recv.at[f, k], device_id=dev, device_id_type=MESH)

    def rows(self, start, n):
        return self.sh(self.p.c * SHARDS + start, n)

    def half(self, f, start, n):
        return self.g.at[f, self.rows(start, n)]

    def done(self, f, start, n):
        return self.out.at[f, self.rows(start, n)]

    def land(self, f, start, n):
        return self.l.at[f, self.sh(start, n)]

    def added(self, f, start, n, off):
        return lambda: add_into(self.g, (f, self.rows(start, n)), self.l[f, self.sh(off, n)])

    def core(self, f):
        p = self.p
        slot = f % self.lc.shape[0]
        src = self.g.at[f, self.sh((1 - p.c) * SHARDS, SHARDS)]
        return [(None, None, self.copy(f, CORE, src, self.lc.at[slot], p.pair("c")),
                 lambda: add_into(self.g, (f, self.rows(0, SHARDS)), self.lc[slot]))]

    def regions(self, path):
        base, n, out = 0, SHARDS, {}
        for axis in path:
            out[axis] = (base, n)
            n = n // (LINE if axis == "z" else PAIR)
            base = base + getattr(self.p, axis) * n
        out["end"] = (base, n)
        return out

    def pair(self, f, path, axis):
        base, n = self.regions(path)[axis]
        mine, off, m = getattr(self.p, axis), LAND[path][axis], n // 2
        k = {"x": X, "y": Y}[axis]
        return [(None, None, self.copy(f, k, self.half(f, base + (1 - mine) * m, m), self.land(f, off, m), self.p.pair(axis)),
                 self.added(f, base + mine * m, m, off))]

    def line(self, f, path, k):
        base, n = self.regions(path)["z"]
        z, m = self.p.z, n // LINE
        off = LAND[path]["z"]
        above, below = off + (LINE - 1 - k) * m, off + (1 + k) * m
        inside = lambda p: base + jnp.clip(p, 0, LINE - 1) * m
        up = self.copy(f, UP + k, self.half(f, inside(z + LINE - k), m), self.land(f, above, m), self.p.up())
        down = self.copy(f, DOWN + k, self.half(f, inside(z - LINE + k), m), self.land(f, below, m), self.p.down())
        return [((z < LINE - 1) & (z <= k - 1), (z > 0) & (z <= k), up, self.added(f, inside(z + LINE - 1 - k), m, above)),
                ((z > 0) & (z >= LINE - k), (z < LINE - 1) & (z >= LINE - 1 - k), down, self.added(f, inside(z - LINE + 1 + k), m, below))]

    def pair_back(self, f, path, axis):
        base, n = self.regions(path)[axis]
        at, m = base + getattr(self.p, axis) * (n // 2), n // 2
        k = {"x": X_BACK, "y": Y_BACK}[axis]
        ref = self.done(f, at, m)
        if axis == path[-1]:
            src = self.half(f, at, m)
            return [(None, None, self.copy(f, k, src, ref, self.p.pair(axis)), None),
                    (None, None, pltpu.make_async_copy(src, ref, self.kept.at[f]), None)]
        return [(None, None, self.copy(f, k, ref, ref, self.p.pair(axis)), None)]

    def line_back(self, f, path, k):
        base, n = self.regions(path)["z"]
        z, m = self.p.z, n // LINE
        inside = lambda p: self.done(f, base + jnp.clip(p, 0, LINE - 1) * m, m)
        up, down = inside(z + 1 - k), inside(z + k - 1)
        return [((z < LINE - 1) & (z >= k - 1), (z > 0) & (z >= k), self.copy(f, UP_BACK + k, up, up, self.p.up()), None),
                ((z > 0) & (z <= LINE - k), (z < LINE - 1) & (z <= LINE - 1 - k), self.copy(f, DOWN_BACK + k, down, down, self.p.down()), None)]

    def core_back(self, f):
        ref = self.done(f, 0, SHARDS)
        return [(None, None, self.copy(f, CORE_BACK, ref, ref, self.p.pair("c")), None)]

    def steps(self, path):
        seq = [self.core]
        for axis in path:
            if axis == "z":
                seq += [functools.partial(self.line, path=path, k=k) for k in range(1, LINE)]
            else:
                seq.append(functools.partial(self.pair, path=path, axis=axis))
        for axis in path[::-1]:
            if axis == "z":
                seq += [functools.partial(self.line_back, path=path, k=k) for k in range(1, LINE)]
            else:
                seq.append(functools.partial(self.pair_back, path=path, axis=axis))
        return seq + [self.core_back]

    def run_stage(self, f, s, path):
        seq = self.steps(path)
        if s > 0:
            for sends, gets, cp, then in seq[s - 1](f):
                if sends is None:
                    cp.wait()
                    if then is not None:
                        then()
                    continue
                pl.when(sends)(cp.wait_send)

                @pl.when(gets)
                def _():
                    cp.wait_recv()
                    if then is not None:
                        then()
        if s < len(seq):
            for sends, gets, cp, then in seq[s](f):
                if sends is None:
                    cp.start()
                else:
                    pl.when(sends)(cp.start)

    def step(self, i, last, paths, offsets):
        n = len(offsets)
        for s in range(n - 1, -1, -1):
            f = i - offsets[s]

            def go(f=f, s=s):
                if s in (0, n - 1):
                    self.run_stage(f, s, "xzy")
                    return
                for path, takes in paths(self.p.c, f):
                    @pl.when(takes)
                    def _():
                        self.run_stage(f, s, path)
            pl.when((f >= 0) & (f < last))(go)


STAGES = 2 * (2 + LINE) + 1


def paths(core, f):
    return [("xzy", core == 0), ("yzx", core == 1)]


OFFSETS = [0, 1] + [2 * s - 1 for s in range(2, STAGES - 1)] + [2 * STAGES - 4]
CORE_SLOTS = 4
T_OFFSETS = [0, 1, 3, 4, 6, 7, 9, 10, 12, 13, 15]
CHUNK = 256
SMALL = 16


def mm(a, b, ca=1, cb=0):
    return lax.dot_general(a, b, (((ca,), (cb,)), ((), ())), preferred_element_type=f32)


def gelu(v):
    return v * (0.5 * (1.0 + jnp.tanh(GELU_A * v * (1.0 + GELU_B * (v * v)))))


def gelu_both(v):
    sq = v * v
    t = jnp.tanh(GELU_A * v * (1.0 + GELU_B * sq))
    h = 0.5 * (1.0 + t)
    return v * h, h + 0.5 * v * (1.0 - t * t) * (GELU_A * (1.0 + 3.0 * GELU_B * sq))


def centred(v):
    c = v - jnp.mean(v, -1, keepdims=True)
    return c, lax.rsqrt(jnp.mean(c * c, -1, keepdims=True) + EPS)


def norm_back(c, rs, u):
    xh = c * rs
    return (u - jnp.mean(u, -1, keepdims=True) - xh * jnp.mean(u * xh, -1, keepdims=True)) * rs


def colsum(v):
    return jnp.sum(v, 0, keepdims=True)


def up16(n):
    return -(-n // 16) * 16


def up128(n):
    return -(-n // 128) * 128


class Sizes:
    def __init__(self, x_lo, x_hi, w_tok1_lo, w_chan_in):
        self.slots, self.q, self.d = x_lo.shape
        self.imgs = self.slots // 4
        self.qh = x_hi.shape[1]
        self.p, self.ph = 4 * self.q, 4 * self.qh
        self.ks = w_tok1_lo.shape[0]
        self.k = 4 * self.ks
        self.ff = w_chan_in.shape[1]
        self.chunks = self.ff // CHUNK
        self.pr = up16(self.p)
        self.own = 2 * self.qh
        self.hi0 = self.imgs * self.pr
        self.rows = self.hi0 + self.own
        self.half_rows = CHUNK * (self.d // 256)
        self.hb = -(-self.ph // 256)
        self.blocks = 2 + 2 * self.hb


def kernel(
    S,
    x_lo, x_hi, cot_lo, cot_hi, counts, w1l, b1l, w2l, b2l, w1h, b1h, w2h, b2h, w_in, w_out, b_in, b_out, gain1, shift1, gain2, shift2,
    out_lo, out_hi, grad_lo, grad_hi, g_sum, t_sum, s_sum,
    xl, xh, cl, ch, wg, bl, bho, bh, w2t_lo, w1_lo, w2t_hi, w1_hi, bcol, bcols, brow, af, nb, nh, n2, ct, tmp, gmh, hid, gp, winv, woutv,
    g, g_core, g_land, t, t_core, t_land, gw1, gw2, gb, sv, s1, s2,
    lo_send, lo_recv, hi_send, hi_recv, w_send, w_recv, ring_send, ring_recv, g_send, g_recv, t_send, t_recv,
    s_send, s_recv, local, g_kept, t_kept,
):
    p = Place()
    y, c = p.y, p.c
    m = y * 2 + c
    dpi = p.z * PAIR + p.x
    peers = [(y, 1 - c), (1 - y, c), (1 - y, 1 - c)]
    d = S.d

    def dev(yy, cc):
        return p.at(y=yy, c=cc)

    def rcopy(src, dst, send, recv, to):
        return pltpu.make_async_remote_copy(src, dst, send, recv, device_id=to, device_id_type=MESH)

    def dp_dev(k):
        i = (dpi + k) % (LINE * PAIR)
        return p.at(z=i // PAIR, x=i % PAIR)

    sem = pltpu.get_barrier_semaphore()
    for yy, cc in peers:
        pl.semaphore_signal(sem, inc=1, device_id=dev(yy, cc), device_id_type=MESH)
    for k in range(1, LINE * PAIR):
        pl.semaphore_signal(sem, inc=1, device_id=dp_dev(k), device_id_type=MESH)
    pl.semaphore_wait(sem, 3 + LINE * PAIR - 1)

    def lo_out(kind, i, src, dst):
        res = []
        for j, (yy, cc) in enumerate(peers):
            mm_ = yy * 2 + cc
            res.append(rcopy(src.at[S.imgs * mm_ + i], dst.at[m, i], lo_send.at[kind, j, i], lo_recv.at[kind, m, i], dev(yy, cc)))
        return res

    def lo_in(kind, i, dst):
        return [rcopy(dst.at[yy * 2 + cc, i], dst.at[yy * 2 + cc, i], lo_send.at[kind, j, i], lo_recv.at[kind, yy * 2 + cc, i], dev(yy, cc)) for j, (yy, cc) in enumerate(peers)]

    def lo_local(kind, i, src, dst):
        return pltpu.make_async_copy(src.at[S.imgs * m + i], dst.at[m, i], local.at[kind, i])

    def lo_back(kind, i, src, dst):
        return [rcopy(src.at[yy * 2 + cc, i], dst.at[S.imgs * m + i], lo_send.at[kind, j, i], lo_recv.at[kind, m, i], dev(yy, cc)) for j, (yy, cc) in enumerate(peers)]

    def lo_back_in(kind, i, dst):
        return [rcopy(dst.at[S.imgs * (yy * 2 + cc) + i], dst.at[S.imgs * (yy * 2 + cc) + i], lo_send.at[kind, j, i], lo_recv.at[kind, yy * 2 + cc, i], dev(yy, cc)) for j, (yy, cc) in enumerate(peers)]

    def lo_back_local(kind, i, src, dst):
        return pltpu.make_async_copy(src.at[m, i], dst.at[S.imgs * m + i], local.at[kind, i])

    def hi_out(kind, src, dst):
        res = []
        for h in range(2):
            mine = (y == h) & (c == y)
            ref = src.at[h] if src.shape[0] == 2 and len(src.shape) == 3 else src
            res.append((mine, rcopy(ref, dst.at[c], hi_send.at[kind, h], hi_recv.at[kind, c], dev(h, y)),
                        pltpu.make_async_copy(ref, dst.at[c], local.at[kind, S.imgs])))
        return res

    def hi_in(kind, dst):
        res = []
        for j in range(2):
            mine = (y == c) & (c == j)
            res.append((mine, rcopy(dst.at[j], dst.at[j], hi_send.at[kind, j], hi_recv.at[kind, j], dev(c, j))))
        return res

    def hi_back(kind, src, dst):
        res = []
        for j in range(2):
            mine = (y == c) & (c == j)
            res.append((mine, rcopy(src.at[j], dst.at[y], hi_send.at[kind, j], hi_recv.at[kind, y], dev(c, j)),
                        pltpu.make_async_copy(src.at[j], dst.at[y], local.at[kind, S.imgs])))
        return res

    def hi_back_in(kind, dst):
        res = []
        for h in range(2):
            mine = (y == h) & (c == y)
            res.append((mine, rcopy(dst.at[h], dst.at[h], hi_send.at[kind, h], hi_recv.at[kind, h], dev(h, y))))
        return res

    def start(copies):
        for cp in copies:
            cp.start()

    def start_hi(copies):
        for mine, remote, here in copies:
            pl.when(mine)(here.start)
            pl.when(jnp.logical_not(mine))(remote.start)

    def sent_hi(copies):
        for mine, remote, here in copies:
            pl.when(mine)(here.wait)
            pl.when(jnp.logical_not(mine))(remote.wait_send)

    def got_hi(copies):
        for mine, remote in copies:
            pl.when(jnp.logical_not(mine))(remote.wait_recv)

    my = (1 - y) * 2 + c

    def across(v, lanes):
        n = v.shape[0]
        return jnp.broadcast_to(v[...].astype(f32).reshape(1, n), (lanes, n)).T.astype(bf16)

    start_hi(hi_out(0, x_hi, xh))
    wg[m] = jnp.zeros((S.blocks, S.ks, 256), bf16)
    wg[m, 0, :, 128:256] = across(b1l, 128)
    wg[m, 1 + S.hb, :, 128:256] = across(b1h, 128)
    wg[m, 0, :, 0:S.pr] = jnp.zeros((S.ks, S.pr), bf16)
    wg[m, 0, :, 0:S.p] = w1l[...]
    wg[m, 1, :, 0:S.p] = w2l[...]
    for j in range(S.hb):
        n = min(256, S.ph - 256 * j)
        wg[m, 2 + j, :, 0:n] = w1h[:, 256 * j:256 * j + n]
        wg[m, 2 + S.hb + j, :, 0:n] = w2h[:, 256 * j:256 * j + n]
    w_y = rcopy(wg.at[m, dpi], wg.at[m, dpi], w_send.at[0], w_recv.at[0], dev(1 - y, c))
    w_y_in = rcopy(wg.at[my, dpi], wg.at[my, dpi], w_send.at[0], w_recv.at[0], dev(1 - y, c))
    w_c = rcopy(wg.at[m], wg.at[m], w_send.at[1], w_recv.at[1], dev(y, 1 - c))
    w_f = rcopy(wg.at[my], wg.at[my], w_send.at[2], w_recv.at[2], dev(y, 1 - c))
    w_d = [rcopy(wg.at[my, dpi], wg.at[my, dpi], w_send.at[6 + k], w_recv.at[7 + dpi], dp_dev(k)) for k in range(1, LINE * PAIR)]
    w_y.start()
    w_c.start()
    bl[m] = across(b2l, 128)
    bias_out = [rcopy(bl.at[m], bl.at[m], w_send.at[3 + j], w_recv.at[3 + m], dev(yy, cc)) for j, (yy, cc) in enumerate(peers)]
    start(bias_out)
    bho[...] = across(b2h, 128)
    bias_hi_out = hi_out(4, bho, bh)
    start_hi(bias_hi_out)
    for i in range(S.imgs):
        start(lo_out(0, i, x_lo, xl))
        lo_local(0, i, x_lo, xl).start()
    start_hi(hi_out(1, cot_hi, ch))
    for i in range(S.imgs):
        start(lo_out(1, i, cot_lo, cl))
        lo_local(1, i, cot_lo, cl).start()
    load_in = pltpu.make_async_copy(w_in, winv, local.at[4, 1])
    load_out = pltpu.make_async_copy(w_out, woutv, local.at[4, 2])
    load_in.start()
    load_out.start()

    def line_of(v):
        return v[...].astype(f32).reshape(1, v.shape[0])

    gv1, sv1 = line_of(gain1), line_of(shift1)
    gv2, sv2 = line_of(gain2), line_of(shift2)
    brow[...] = line_of(b_in)
    hi = pl.ds(S.hi0, S.own)
    own = pl.ds(pl.multiple_of(c * S.own, 16), S.own)

    def img(i):
        return pl.ds(pl.multiple_of(i * S.pr, 16), S.pr)

    def gather_rows(block, i):
        for s in range(4):
            tmp[s * S.q:(s + 1) * S.q, :] = block[s, i].astype(f32)
        if S.pr > S.p:
            tmp[S.p:S.pr, :] = jnp.zeros((S.pr - S.p, d), f32)

    def scatter_rows(block, i):
        for s in range(4):
            block[s, i] = tmp[s * S.q:(s + 1) * S.q, :].astype(bf16)

    sv[...] = jnp.zeros_like(sv)
    t[...] = jnp.zeros_like(t)
    gw1[...] = jnp.zeros_like(gw1)
    gw2[...] = jnp.zeros_like(gw2)

    got_hi(hi_in(0, xh))
    sent_hi(hi_out(0, x_hi, xh))
    v = xh[...].reshape(S.own, d).astype(f32)
    cen, rs = centred(v)
    n = (cen * rs * gv1 + sv1).astype(bf16)
    nb[hi, :] = n
    nh[own, :] = n
    af[hi, :] = v
    nh_copy = rcopy(nh.at[own], nh.at[own], ring_send.at[0], ring_recv.at[0], dev(y, 1 - c))
    nh_copy.start()

    w_y.wait_send()
    w_y_in.wait_recv()
    start(w_d)
    for k in range(1, LINE * PAIR):
        i = (dpi + k) % (LINE * PAIR)
        w_d[k - 1].wait_send()
        rcopy(wg.at[my, i], wg.at[my, i], w_send.at[6 + k], w_recv.at[7 + i], dp_dev(k)).wait_recv()
    w_f.start()
    w_c.wait()
    w_f.wait_send()
    w_far = rcopy(wg.at[(1 - y) * 2 + 1 - c], wg.at[(1 - y) * 2 + 1 - c], w_send.at[2], w_recv.at[2], dev(y, 1 - c))
    w_far.wait_recv()

    def block(b, n):
        return wg[:, b, :, 0:n].reshape(S.k, n)

    def w1t_lo():
        return block(0, S.pr)

    def w2_lo():
        return block(1, S.pr)

    def bias_of(b):
        return wg[:, b, :, 128:256].reshape(S.k, 128).astype(f32)[:, 127:128]

    spans = [(256 * j, min(256, S.ph - 256 * j)) for j in range(S.hb)]

    def mm_hi(first, rows_of):
        return functools.reduce(jnp.add, [mm(block(first + j, n), rows_of[at:at + n, :]) for j, (at, n) in enumerate(spans)])

    for k in range(2):
        bcols[k] = jnp.broadcast_to(bias_of(k * (1 + S.hb)), (S.k, 128))

    def b1_lo():
        return bcols[0, :, 0:1]

    def b1_hi():
        return bcols[1, :, 0:1]

    w1_lo[...] = w1t_lo().T
    w2t_lo[...] = w2_lo().T
    for j, (at, n) in enumerate(spans):
        w1_hi[at:at + n, :] = block(2 + j, n).T
        w2t_hi[at:at + n, :] = block(2 + S.hb + j, n).T
    for j, (yy, cc) in enumerate(peers):
        bias_out[j].wait_send()
        s = yy * 2 + cc
        rcopy(bl.at[s], bl.at[s], w_send.at[3 + j], w_recv.at[3 + s], dev(yy, cc)).wait_recv()
    got_hi(hi_in(4, bh))
    sent_hi(bias_hi_out)
    bcol[...] = jnp.zeros_like(bcol)
    for s in range(4):
        bcol[s * S.q:(s + 1) * S.q, :] = bl[s].astype(f32)

    def fwd_lo(i, carry):
        for cp in lo_in(0, i, xl):
            cp.wait_recv()
        lo_local(0, i, x_lo, xl).wait()
        gather_rows(xl, i)
        v = tmp[...]
        cen, rs = centred(v)
        n = (cen * rs * gv1 + sv1).astype(bf16)
        nb[img(i), :] = n
        ht = gelu(mm(w1t_lo(), n) + b1_lo()).astype(bf16)
        af[img(i), :] = v + (mm(w2t_lo[...], ht) + bcol[:, 0:1])
        return carry

    lax.fori_loop(0, S.imgs, fwd_lo, 0)
    nh_copy.wait()
    ht = gelu(mm_hi(2, nh) + b1_hi()).astype(bf16)
    bcol_hi = bh[...].reshape(S.own, 128).astype(f32)[:, 0:1]
    af[hi, :] = af[hi, :] + (mm(w2t_hi[own, :], ht) + bcol_hi)

    def norm_two(rows):
        cen, rs = centred(af[rows, :])
        n2[rows, :] = (cen * rs * gv2 + sv2).astype(bf16)

    norm_two(hi)

    def norm_lo(i, carry):
        norm_two(img(i))
        return carry

    lax.fori_loop(0, S.imgs, norm_lo, 0)

    def live_lo(i):
        return jnp.where(S.imgs * m + i < counts[0, 0], 1.0, 0.0).astype(f32)

    live_hi = jnp.where(y < counts[0, 1], 1.0, 0.0).astype(f32)
    got_hi(hi_in(1, ch))
    sent_hi(hi_out(1, cot_hi, ch))
    ct[hi, :] = (ch[...].reshape(S.own, d).astype(f32) * live_hi).astype(bf16)

    def cot_rows(i, carry):
        for cp in lo_in(1, i, cl):
            cp.wait_recv()
        lo_local(1, i, cot_lo, cl).wait()
        gather_rows(cl, i)
        ct[img(i), :] = (tmp[...] * live_lo(i)).astype(bf16)
        return carry

    lax.fori_loop(0, S.imgs, cot_rows, 0)
    for kind, src, dst in ((0, x_lo, xl), (1, cot_lo, cl)):
        for i in range(S.imgs):
            for cp in lo_out(kind, i, src, dst):
                cp.wait_send()
    load_in.wait()
    load_out.wait()

    def channel(f):
        cols = pl.ds(pl.multiple_of(f * CHUNK, CHUNK), CHUNK)
        h, slope = gelu_both(mm(n2[...], winv[:, cols]) + brow[:, cols])
        hb = h.astype(bf16)
        hid[:, cols] = hb
        gpre = (mm(ct[...], woutv[cols, :], 1, 1) * slope).astype(bf16)
        gp[:, cols] = gpre
        gb[:, cols] = colsum(gpre.astype(f32))
        g[f, 0:d, :] = mm(n2[...], gpre, 0, 0).astype(bf16)
        grad = mm(hb, ct[...], 0, 0)
        for j in range(d // 256):
            g[f, S.half_rows + CHUNK * j:S.half_rows + CHUNK * (j + 1), :] = grad[:, 256 * j:256 * (j + 1)].astype(bf16)

    bo = line_of(b_out)

    def channel_back(rows, live):
        a = af[rows, :]
        out = (a + mm(hid[rows, :], woutv[...]) + bo) * live
        gn = mm(gp[rows, :], winv[...], 1, 1)
        cen, rs = centred(a)
        c_rows = ct[rows, :].astype(f32)
        grad = c_rows + norm_back(cen, rs, gn * gv2)
        sv[0:1, :] += colsum(c_rows)
        sv[1:2, :] += colsum(gn * (cen * rs))
        sv[2:3, :] += colsum(gn)
        af[rows, :] = grad
        n2[rows, :] = grad.astype(bf16)
        return out

    def back_hi():
        out = channel_back(hi, live_hi)
        ch[...] = out.astype(bf16).reshape(2, S.qh, d)
        gmh[own, :] = n2[hi, :]
        gm_copy.start()

    gm_copy = rcopy(gmh.at[own], gmh.at[own], ring_send.at[1], ring_recv.at[1], dev(y, 1 - c))

    def back_lo(i):
        tmp[...] = channel_back(img(i), live_lo(i))
        scatter_rows(cl, i)

    ones = jnp.ones((8, d), bf16)

    def first_norm_back(v, gn, rows):
        cen, rs = centred(v)
        sv[3:4, :] += colsum(gn * (cen * rs))
        sv[4:5, :] += colsum(gn)
        return af[rows, :] + norm_back(cen, rs, gn * gv1)

    def token_lo(i):
        n = nb[img(i), :]
        gm = n2[img(i), :]
        h, slope = gelu_both(mm(w1t_lo(), n) + b1_lo())
        gw2[:, 0:S.pr] += mm(h.astype(bf16), gm, 1, 1)
        gpt = (mm(w2_lo(), gm) * slope).astype(bf16)
        gw1[:, 0:S.pr] += mm(gpt, n, 1, 1)
        sv[9:10, 0:S.k] += mm(ones, gpt, 1, 1)[0:1]
        sv[10:11, 0:S.pr] += mm(ones, gm, 1, 1)[0:1]
        gn = mm(w1_lo[...], gpt)
        gather_rows(xl, i)
        tmp[...] = first_norm_back(tmp[...], gn, img(i))
        scatter_rows(xl, i)
        start(lo_back(3, i, xl, grad_lo))
        lo_back_local(3, i, xl, grad_lo).start()

    def token_hi():
        gm_copy.wait()
        n = nb[hi, :]
        gm = n2[hi, :]
        h, slope = gelu_both(mm_hi(2, nh) + b1_hi())
        ga2 = mm(h.astype(bf16), gmh[...], 1, 1) * 0.5
        gpt = (mm_hi(2 + S.hb, gmh) * slope).astype(bf16)
        ga1 = mm(gpt, nh[...], 1, 1) * 0.5
        sv[11:12, 0:S.k] += mm(ones, gpt, 1, 1)[0:1] * 0.5
        sv[pl.ds(12 + c, 1), 0:S.own] = mm(ones, gm, 1, 1)[0:1]
        gn = mm(w1_hi[own, :], gpt)
        grad = first_norm_back(xh[...].reshape(S.own, d).astype(f32), gn, hi)
        xh[...] = grad.astype(bf16).reshape(2, S.qh, d)
        start_hi(hi_back(3, xh, grad_hi))
        for j in range(S.ff // d):
            sv[5 + j:6 + j, :] = gb[:, d * j:d * (j + 1)]
        s1[m] = sv[...]
        start(s1_out)
        for ks in range(4):
            k0, yy, cc = ks * S.ks, ks // 2, ks % 2

            def put(j, v, n=256):
                row = (cc * SHARDS + 2 * j + yy) * S.ks
                t[0, row:row + S.ks, 0:n] = v.astype(bf16)

            put(0, gw1[k0:k0 + S.ks, :])
            put(1, gw2[k0:k0 + S.ks, :])
            for j in range(S.hb):
                n = min(256, S.ph - 256 * j)
                put(2 + j, ga1[k0:k0 + S.ks, 256 * j:256 * j + n], n)
                put(2 + S.hb + j, ga2[k0:k0 + S.ks, 256 * j:256 * j + n], n)

    s1_out = [rcopy(s1.at[m], s1.at[m], s_send.at[j], s_recv.at[m], dev(yy, cc)) for j, (yy, cc) in enumerate(peers)]
    s2_out = [rcopy(s2.at[dpi], s2.at[dpi], s_send.at[3 + k], s_recv.at[4 + dpi], dp_dev(k)) for k in range(1, LINE * PAIR)]

    ar = AllReduce(p, g, g_core, g_land, g_sum, g_send, g_recv, g_kept)
    art = TokenSum(p, t, t_core, t_land, t_sum, t_send, t_recv, t_kept)
    nc = S.chunks
    b0 = nc + 1 + S.imgs
    t0 = b0 + S.imgs

    def send_out(k):
        start(lo_back(2, k, cl, out_lo))
        lo_back_local(2, k, cl, out_lo).start()

    def step(i, carry):
        pl.when(i < nc)(lambda: channel(i))
        pl.when(i == nc)(back_hi)
        pl.when((i > nc) & (i < b0))(lambda: back_lo(i - nc - 1))
        pl.when((i >= b0) & (i < t0))(lambda: token_lo(i - b0))
        pl.when(i == t0)(token_hi)
        pl.when(i == t0 + 2)(small_sums)
        pl.when(i == t0 + 2)(lambda: start_hi(hi_back(2, ch, out_hi)))
        for k in range(S.imgs):
            pl.when(i == t0 + 4 + 2 * k)(functools.partial(send_out, k))
        ar.step(i, nc, paths, OFFSETS)
        art.step(i - t0, T_OFFSETS)
        return carry

    def small_sums():
        for j, (yy, cc) in enumerate(peers):
            s = yy * 2 + cc
            s1_out[j].wait_send()
            rcopy(s1.at[s], s1.at[s], s_send.at[j], s_recv.at[s], dev(yy, cc)).wait_recv()
        s2[dpi] = s1[0] + s1[1] + s1[2] + s1[3]
        start(s2_out)

    lax.fori_loop(0, max(nc + OFFSETS[-1], t0 + 1 + T_OFFSETS[-1]), step, 0)
    for k in range(1, LINE * PAIR):
        i = (dpi + k) % (LINE * PAIR)
        s2_out[k - 1].wait_send()
        rcopy(s2.at[i], s2.at[i], s_send.at[3 + k], s_recv.at[4 + i], dp_dev(k)).wait_recv()
    total = s2[0]
    for i in range(1, LINE * PAIR):
        total = total + s2[i]
    s_sum[...] = total

    for kind, src, src_hi, dst, dst_hi in ((2, cl, ch, out_lo, out_hi), (3, xl, xh, grad_lo, grad_hi)):
        for i in range(S.imgs):
            for cp in lo_back(kind, i, src, dst):
                cp.wait_send()
            for cp in lo_back_in(kind, i, dst):
                cp.wait_recv()
            lo_back_local(kind, i, src, dst).wait()
        sent_hi(hi_back(kind, src_hi, dst_hi))
        got_hi(hi_back_in(kind, dst_hi))


def mixer(S, args):
    V = pl.BlockSpec(memory_space=pltpu.VMEM)
    A = pl.BlockSpec(memory_space=pl.ANY)
    M = pl.BlockSpec(memory_space=pltpu.SMEM)
    sds = jax.ShapeDtypeStruct
    d, dma = S.d, pltpu.SemaphoreType.DMA
    nc = S.chunks
    unit = 2 * S.half_rows // (2 * SHARDS)
    scratch = [
        pltpu.VMEM((4, S.imgs, S.q, d), bf16), pltpu.VMEM((2, S.qh, d), bf16),
        pltpu.VMEM((4, S.imgs, S.q, d), bf16), pltpu.VMEM((2, S.qh, d), bf16),
        pltpu.VMEM((4, S.blocks, S.ks, 256), bf16), pltpu.VMEM((4, S.q, 128), bf16), pltpu.VMEM((S.qh, 128), bf16), pltpu.VMEM((2, S.qh, 128), bf16),
        pltpu.VMEM((S.pr, S.k), bf16), pltpu.VMEM((S.pr, S.k), bf16), pltpu.VMEM((S.ph, S.k), bf16), pltpu.VMEM((S.ph, S.k), bf16),
        pltpu.VMEM((S.pr, 128), f32), pltpu.VMEM((2, S.k, 128), f32), pltpu.VMEM((1, S.ff), f32),
        pltpu.VMEM((S.rows, d), f32), pltpu.VMEM((S.rows, d), bf16), pltpu.VMEM((S.ph, d), bf16), pltpu.VMEM((S.rows, d), bf16),
        pltpu.VMEM((S.rows, d), bf16), pltpu.VMEM((S.pr, d), f32), pltpu.VMEM((S.ph, d), bf16),
        pltpu.VMEM((S.rows, S.ff), bf16), pltpu.VMEM((S.rows, S.ff), bf16), pltpu.VMEM((d, S.ff), bf16), pltpu.VMEM((S.ff, d), bf16),
        pltpu.VMEM((nc, 2 * SHARDS * unit, 256), bf16), pltpu.VMEM((CORE_SLOTS, SHARDS * unit, 256), bf16), pltpu.VMEM((nc, LANDED * unit, 256), bf16),
        pltpu.VMEM((1, 2 * SHARDS * S.ks, 256), bf16), pltpu.VMEM((1, SHARDS * S.ks, 256), bf16), pltpu.VMEM((1, LANDED * S.ks, 256), bf16),
        pltpu.VMEM((S.k, 256), f32), pltpu.VMEM((S.k, 256), f32), pltpu.VMEM((1, S.ff), f32),
        pltpu.VMEM((SMALL, d), f32), pltpu.VMEM((4, SMALL, d), f32), pltpu.VMEM((LINE * PAIR, SMALL, d), f32),
        dma((4, 3, S.imgs)), dma((4, 4, S.imgs)), dma((5, 2)), dma((5, 2)), dma((14,)), dma((15,)), dma((2,)), dma((2,)),
        dma((nc, NSEM)), dma((nc, NSEM)), dma((1, NSEM)), dma((1, NSEM)), dma((11,)), dma((12,)), dma((5, S.imgs + 1)), dma((nc,)), dma((1,)),
    ]
    return pl.pallas_call(
        functools.partial(kernel, S),
        out_shape=(
            sds((S.slots, S.q, d), bf16), sds((2, S.qh, d), bf16), sds((S.slots, S.q, d), bf16), sds((2, S.qh, d), bf16),
            sds((nc, 2 * S.half_rows, 256), bf16), sds((1, S.blocks * S.ks, 256), bf16), sds((SMALL, d), f32),
        ),
        in_specs=[A, A, A, A, M] + [V] * 8 + [A, A] + [V] * 6,
        out_specs=(A, A, A, A, A, A, V),
        scratch_shapes=scratch,
        compiler_params=pltpu.CompilerParams(collective_id=0, has_side_effects=True, vmem_limit_bytes=63 * 1024 * 1024),
    )(*args)


class TokenSum(AllReduce):
    def part(self, i):
        return self.out.at[0, self.sh(i, 1)]

    def line_back(self, f, path, k):
        z, base = self.p.z, self.p.x * LINE
        inside = lambda p: self.part(base + jnp.clip(p, 0, LINE - 1))
        up, down = inside(z + 1 - k), inside(z + k - 1)
        up_src, down_src, more = up, down, []
        if k == 1:
            up_src = down_src = self.half(f, (base + z) * PAIR + self.p.y, 1)
            more = [(None, None, pltpu.make_async_copy(up_src, up, self.kept.at[f]), None)]
        return [((z < LINE - 1) & (z >= k - 1), (z > 0) & (z >= k), self.copy(f, UP_BACK + k, up_src, up, self.p.up()), None),
                ((z > 0) & (z <= LINE - k), (z < LINE - 1) & (z <= LINE - 1 - k), self.copy(f, DOWN_BACK + k, down_src, down, self.p.down()), None)] + more

    def x_back(self, f):
        ref = self.out.at[0, self.sh(self.p.x * LINE, LINE)]
        return [(None, None, self.copy(f, X_BACK, ref, ref, self.p.pair("x")), None)]

    def steps(self, path):
        there = super().steps(path)[:2 + LINE]
        return there + [functools.partial(self.line_back, path=path, k=k) for k in range(1, LINE)] + [self.x_back]

    def step(self, i, offsets):
        for s in range(len(offsets)):
            pl.when(i == offsets[s])(functools.partial(self.run_stage, 0, s, "xzy"))


def finish(S, out_lo, out_hi, grad_lo, grad_hi, g, t, s):
    d = S.d
    sds = jax.ShapeDtypeStruct

    def place(ol, oh, gl, gh, g_ref, t_ref, s_ref, *outs):
        (o_lo, o_hi, r_lo, r_hi, l1g, l1b, w1l, b1l, w2l, b2l, w1h, b1h, w2h, b2h, l2g, l2b, w_in, b_in, w_out, b_out) = outs
        m = lax.axis_index("mp")
        w_in[...] = g_ref[0, 0:d, :].astype(f32)
        for j in range(d // 256):
            w_out[:, 256 * j:256 * (j + 1)] = g_ref[0, S.half_rows + CHUNK * j:S.half_rows + CHUNK * (j + 1), :].astype(f32)
        o_lo[...] = ol[...]
        r_lo[...] = gl[...].astype(f32)

        @pl.when(pl.program_id(0) == 0)
        def _():
            o_hi[...] = oh[...]
            r_hi[...] = gh[...].astype(f32)
            w1l[...] = t_ref[0, :, 0:S.p].astype(f32)
            w2l[...] = t_ref[1, :, 0:S.p].astype(f32)
            for j in range(S.hb):
                n = min(256, S.ph - 256 * j)
                w1h[:, 256 * j:256 * j + n] = t_ref[2 + j, :, 0:n].astype(f32)
                w2h[:, 256 * j:256 * j + n] = t_ref[2 + S.hb + j, :, 0:n].astype(f32)
            for i, o in ((0, b_out), (1, l2g), (2, l2b), (3, l1g), (4, l1b)):
                o[...] = s_ref[i, :]
            for j in range(S.ff // d):
                b_in[d * j:d * (j + 1)] = s_ref[5 + j, :]
            for j in range(4):
                @pl.when(m == j)
                def _():
                    b1l[...] = s_ref[9, S.ks * j:S.ks * (j + 1)]
                    b2l[...] = s_ref[10, S.q * j:S.q * (j + 1)]
                    b1h[...] = s_ref[11, S.ks * j:S.ks * (j + 1)]
                    b2h[...] = s_ref[12 + j // 2, S.qh * (j % 2):S.qh * (j % 2 + 1)]

    def whole(v):
        return pl.BlockSpec(v.shape, lambda i: (0,) * len(v.shape))

    image = pl.BlockSpec((S.slots // S.chunks, S.q, d), lambda i: (i, 0, 0))
    vec = lambda n: sds((n,), f32)
    shapes = [
        sds(out_lo.shape, bf16), sds(out_hi.shape, bf16), sds(out_lo.shape, f32), sds(out_hi.shape, f32), vec(d), vec(d),
        sds((S.ks, S.p), f32), vec(S.ks), sds((S.ks, S.p), f32), vec(S.q), sds((S.ks, S.ph), f32), vec(S.ks), sds((S.ks, S.ph), f32), vec(S.qh),
        vec(d), vec(d), sds((d, S.ff), f32), vec(S.ff), sds((S.ff, d), f32), vec(d),
    ]
    outs = [whole(v) for v in shapes]
    outs[0] = outs[2] = image
    outs[16] = pl.BlockSpec((d, CHUNK), lambda i: (0, i))
    outs[18] = pl.BlockSpec((CHUNK, d), lambda i: (i, 0))
    t = t.reshape(S.blocks, S.ks, 256)
    return pl.pallas_call(
        place,
        grid=(S.chunks,),
        out_shape=shapes,
        in_specs=[image, whole(out_hi), image, whole(grad_hi), pl.BlockSpec((1, 2 * S.half_rows, 256), lambda i: (i, 0, 0)), whole(t), whole(s)],
        out_specs=outs,
        compiler_params=pltpu.CompilerParams(vmem_limit_bytes=63 * 1024 * 1024),
    )(out_lo, out_hi, grad_lo, grad_hi, g, t, s)


def body(
    groups,
    x_lo, x_hi, cot_lo, cot_hi, counts, ln1_gain, ln1_bias, w_tok1_lo, b_tok1_lo, w_tok2_lo, b_tok2_lo, w_tok1_hi, b_tok1_hi,
    w_tok2_hi, b_tok2_hi, ln2_gain, ln2_bias, w_chan_in, b_chan_in, w_chan_out, b_chan_out,
):
    w1_lo, w1_hi = w_tok1_lo.T, w_tok1_hi.T
    S = Sizes(x_lo, x_hi, w1_lo, w_chan_in)
    out_lo, out_hi, grad_lo, grad_hi, g, t, s = mixer(
        S,
        (x_lo, x_hi, cot_lo, cot_hi, counts, w1_lo, b_tok1_lo, w_tok2_lo, b_tok2_lo, w1_hi, b_tok1_hi, w_tok2_hi, b_tok2_hi,
         w_chan_in, w_chan_out, b_chan_in, b_chan_out, ln1_gain, ln1_bias, ln2_gain, ln2_bias),
    )
    if groups is not None:
        g, t, s = lax.psum((g.astype(f32), t.astype(f32), s), "dp", axis_index_groups=groups)
    res = list(finish(S, out_lo, out_hi, grad_lo, grad_hi, g, t, s))
    res[6], res[10] = res[6].T, res[10].T
    return tuple(res)


def solution(mesh):
    blocks = mesh.shape["dp"] // (LINE * PAIR)
    groups = None
    if blocks > 1:
        size = LINE * PAIR
        groups = [[b * size + i for b in range(blocks)] for i in range(size)]
    tokens, rows = P("dp", "mp", None), P("dp", None)
    col, row, vec, rep = P(None, "mp"), P("mp", None), P("mp"), P()
    return jax.shard_map(
        functools.partial(body, groups),
        mesh=mesh,
        in_specs=(tokens,) * 4 + (rows, rep, rep) + (col, vec, row, vec) * 2 + (rep,) * 6,
        out_specs=(tokens,) * 4 + (rep, rep) + (col, vec, row, vec) * 2 + (rep,) * 6,
        check_vma=False,
    )
```

```python
import functools

import jax
import jax.numpy as jnp
from jax import lax
from jax.experimental import pallas as pl
from jax.experimental.pallas import tpu as pltpu
from jax.sharding import PartitionSpec as P

MESH = pl.DeviceIdType.MESH
EPS = 1e-06
GELU_A, GELU_B = 0.7978845608028654, 0.044715
f32, bf16 = jnp.float32, jnp.bfloat16

LINE, PAIR = 4, 2
SHARDS = 16
LAND = {"xzy": dict(x=0, z=8, y=18), "yzx": dict(y=0, z=8, x=18)}
LANDED = 19
CORE, X, Y, UP, DOWN, X_BACK, Y_BACK, UP_BACK, DOWN_BACK, CORE_BACK, NSEM = 0, 1, 2, 2, 5, 9, 10, 10, 13, 17, 18


class Place:
    def __init__(self):
        dp, mp = lax.axis_index("dp"), lax.axis_index("mp")
        self.block = dp // (LINE * PAIR)
        self.z = (dp // PAIR) % LINE
        self.x = dp % PAIR
        self.y = mp // 2
        self.c = mp % 2

    def at(self, z=None, x=None, y=None, c=None):
        z = self.z if z is None else z
        x = self.x if x is None else x
        y = self.y if y is None else y
        c = self.c if c is None else c
        return (self.block * (LINE * PAIR) + z * PAIR + x, y * 2 + c)

    def up(self):
        return self.at(z=jnp.minimum(self.z + 1, LINE - 1))

    def down(self):
        return self.at(z=jnp.maximum(self.z - 1, 0))

    def pair(self, axis):
        return self.at(**{axis: 1 - getattr(self, axis)})


def add_into(ref, idx, *others):
    total = ref[idx].astype(f32)
    for o in others:
        total = total + o.astype(f32)
    ref[idx] = total.astype(bf16)


class AllReduce:
    def __init__(self, place, g, land_core, land, out, send, recv, kept):
        self.p, self.g, self.lc, self.l, self.out, self.send, self.recv, self.kept = place, g, land_core, land, out, send, recv, kept
        self.unit = g.shape[1] // (2 * SHARDS)

    def sh(self, start, n):
        if isinstance(start, int):
            return pl.ds(start * self.unit, n * self.unit)
        return pl.ds(pl.multiple_of(start * self.unit, 16), n * self.unit)

    def copy(self, f, k, src, dst, dev):
        return pltpu.make_async_remote_copy(src, dst, self.send.at[f, k], self.recv.at[f, k], device_id=dev, device_id_type=MESH)

    def rows(self, start, n):
        return self.sh(self.p.c * SHARDS + start, n)

    def half(self, f, start, n):
        return self.g.at[f, self.rows(start, n)]

    def done(self, f, start, n):
        return self.out.at[f, self.rows(start, n)]

    def land(self, f, start, n):
        return self.l.at[f, self.sh(start, n)]

    def added(self, f, start, n, off):
        return lambda: add_into(self.g, (f, self.rows(start, n)), self.l[f, self.sh(off, n)])

    def core(self, f):
        p = self.p
        slot = f % self.lc.shape[0]
        src = self.g.at[f, self.sh((1 - p.c) * SHARDS, SHARDS)]
        return [(None, None, self.copy(f, CORE, src, self.lc.at[slot], p.pair("c")),
                 lambda: add_into(self.g, (f, self.rows(0, SHARDS)), self.lc[slot]))]

    def regions(self, path):
        base, n, out = 0, SHARDS, {}
        for axis in path:
            out[axis] = (base, n)
            n = n // (LINE if axis == "z" else PAIR)
            base = base + getattr(self.p, axis) * n
        out["end"] = (base, n)
        return out

    def pair(self, f, path, axis):
        base, n = self.regions(path)[axis]
        mine, off, m = getattr(self.p, axis), LAND[path][axis], n // 2
        k = {"x": X, "y": Y}[axis]
        return [(None, None, self.copy(f, k, self.half(f, base + (1 - mine) * m, m), self.land(f, off, m), self.p.pair(axis)),
                 self.added(f, base + mine * m, m, off))]

    def line(self, f, path, k):
        base, n = self.regions(path)["z"]
        z, m = self.p.z, n // LINE
        off = LAND[path]["z"]
        above, below = off + (LINE - 1 - k) * m, off + (1 + k) * m
        inside = lambda p: base + jnp.clip(p, 0, LINE - 1) * m
        up = self.copy(f, UP + k, self.half(f, inside(z + LINE - k), m), self.land(f, above, m), self.p.up())
        down = self.copy(f, DOWN + k, self.half(f, inside(z - LINE + k), m), self.land(f, below, m), self.p.down())
        return [((z < LINE - 1) & (z <= k - 1), (z > 0) & (z <= k), up, self.added(f, inside(z + LINE - 1 - k), m, above)),
                ((z > 0) & (z >= LINE - k), (z < LINE - 1) & (z >= LINE - 1 - k), down, self.added(f, inside(z - LINE + 1 + k), m, below))]

    def pair_back(self, f, path, axis):
        base, n = self.regions(path)[axis]
        at, m = base + getattr(self.p, axis) * (n // 2), n // 2
        k = {"x": X_BACK, "y": Y_BACK}[axis]
        ref = self.done(f, at, m)
        if axis == path[-1]:
            src = self.half(f, at, m)
            return [(None, None, self.copy(f, k, src, ref, self.p.pair(axis)), None),
                    (None, None, pltpu.make_async_copy(src, ref, self.kept.at[f]), None)]
        return [(None, None, self.copy(f, k, ref, ref, self.p.pair(axis)), None)]

    def line_back(self, f, path, k):
        base, n = self.regions(path)["z"]
        z, m = self.p.z, n // LINE
        inside = lambda p: self.done(f, base + jnp.clip(p, 0, LINE - 1) * m, m)
        up, down = inside(z + 1 - k), inside(z + k - 1)
        return [((z < LINE - 1) & (z >= k - 1), (z > 0) & (z >= k), self.copy(f, UP_BACK + k, up, up, self.p.up()), None),
                ((z > 0) & (z <= LINE - k), (z < LINE - 1) & (z <= LINE - 1 - k), self.copy(f, DOWN_BACK + k, down, down, self.p.down()), None)]

    def core_back(self, f):
        ref = self.done(f, 0, SHARDS)
        return [(None, None, self.copy(f, CORE_BACK, ref, ref, self.p.pair("c")), None)]

    def steps(self, path):
        seq = [self.core]
        for axis in path:
            if axis == "z":
                seq += [functools.partial(self.line, path=path, k=k) for k in range(1, LINE)]
            else:
                seq.append(functools.partial(self.pair, path=path, axis=axis))
        for axis in path[::-1]:
            if axis == "z":
                seq += [functools.partial(self.line_back, path=path, k=k) for k in range(1, LINE)]
            else:
                seq.append(functools.partial(self.pair_back, path=path, axis=axis))
        return seq + [self.core_back]

    def run_stage(self, f, s, path):
        seq = self.steps(path)
        if s > 0:
            for sends, gets, cp, then in seq[s - 1](f):
                if sends is None:
                    cp.wait()
                    if then is not None:
                        then()
                    continue
                pl.when(sends)(cp.wait_send)

                @pl.when(gets)
                def _():
                    cp.wait_recv()
                    if then is not None:
                        then()
        if s < len(seq):
            for sends, gets, cp, then in seq[s](f):
                if sends is None:
                    cp.start()
                else:
                    pl.when(sends)(cp.start)

    def step(self, i, last, paths, offsets):
        n = len(offsets)
        for s in range(n):
            f = i - offsets[s]

            def go(f=f, s=s):
                if s in (0, n - 1):
                    self.run_stage(f, s, "xzy")
                    return
                for path, takes in paths(self.p.c, f):
                    @pl.when(takes)
                    def _():
                        self.run_stage(f, s, path)
            pl.when((f >= 0) & (f < last))(go)


STAGES = 2 * (2 + LINE) + 1


def paths(core, f):
    return [("xzy", core == 0), ("yzx", core == 1)]


OFFSETS = [0, 1] + [2 * s - 1 for s in range(2, STAGES - 1)] + [2 * STAGES - 4]
CORE_SLOTS = 4
T_OFFSETS = [0, 1, 3, 4, 6, 7, 9, 10, 12, 13, 15]
CHUNK = 256
SMALL = 16


def mm(a, b, ca=1, cb=0):
    return lax.dot_general(a, b, (((ca,), (cb,)), ((), ())), preferred_element_type=f32)


def gelu(v):
    return v * (0.5 * (1.0 + jnp.tanh(GELU_A * v * (1.0 + GELU_B * (v * v)))))


def gelu_both(v):
    sq = v * v
    t = jnp.tanh(GELU_A * v * (1.0 + GELU_B * sq))
    h = 0.5 * (1.0 + t)
    return v * h, h + 0.5 * v * (1.0 - t * t) * (GELU_A * (1.0 + 3.0 * GELU_B * sq))


def centred(v):
    c = v - jnp.mean(v, -1, keepdims=True)
    return c, lax.rsqrt(jnp.mean(c * c, -1, keepdims=True) + EPS)


def norm_back(c, rs, u):
    xh = c * rs
    return (u - jnp.mean(u, -1, keepdims=True) - xh * jnp.mean(u * xh, -1, keepdims=True)) * rs


def colsum(v):
    return jnp.sum(v, 0, keepdims=True)


def up16(n):
    return -(-n // 16) * 16


def up128(n):
    return -(-n // 128) * 128


class Sizes:
    def __init__(self, x_lo, x_hi, w_tok1_lo, w_chan_in):
        self.slots, self.q, self.d = x_lo.shape
        self.imgs = self.slots // 4
        self.qh = x_hi.shape[1]
        self.p, self.ph = 4 * self.q, 4 * self.qh
        self.ks = w_tok1_lo.shape[0]
        self.k = 4 * self.ks
        self.ff = w_chan_in.shape[1]
        self.chunks = self.ff // CHUNK
        self.pr = up16(self.p)
        self.own = 2 * self.qh
        self.hi0 = self.imgs * self.pr
        self.rows = self.hi0 + self.own
        self.half_rows = CHUNK * (self.d // 256)
        self.hb = -(-self.ph // 256)
        self.blocks = 2 + 2 * self.hb


def kernel(
    S,
    x_lo, x_hi, cot_lo, cot_hi, counts, w1l, b1l, w2l, b2l, w1h, b1h, w2h, b2h, w_in, w_out, b_in, b_out, gain1, shift1, gain2, shift2,
    out_lo, out_hi, grad_lo, grad_hi, g_sum, t_sum, s_sum,
    xl, xh, cl, ch, wg, bl, bho, bh, w2t_lo, w1_lo, w2t_hi, w1_hi, bcol, bcols, brow, af, nb, nh, n2, ct, tmp, gmh, hid, gp, winv, woutv,
    g, g_core, g_land, t, t_core, t_land, gw1, gw2, gb, sv, s1, s2,
    lo_send, lo_recv, hi_send, hi_recv, w_send, w_recv, ring_send, ring_recv, g_send, g_recv, t_send, t_recv,
    s_send, s_recv, local, g_kept, t_kept,
):
    p = Place()
    y, c = p.y, p.c
    m = y * 2 + c
    dpi = p.z * PAIR + p.x
    peers = [(y, 1 - c), (1 - y, c), (1 - y, 1 - c)]
    d = S.d

    def dev(yy, cc):
        return p.at(y=yy, c=cc)

    def rcopy(src, dst, send, recv, to):
        return pltpu.make_async_remote_copy(src, dst, send, recv, device_id=to, device_id_type=MESH)

    def dp_dev(k):
        i = (dpi + k) % (LINE * PAIR)
        return p.at(z=i // PAIR, x=i % PAIR)

    sem = pltpu.get_barrier_semaphore()
    for yy, cc in peers:
        pl.semaphore_signal(sem, inc=1, device_id=dev(yy, cc), device_id_type=MESH)
    for k in range(1, LINE * PAIR):
        pl.semaphore_signal(sem, inc=1, device_id=dp_dev(k), device_id_type=MESH)
    pl.semaphore_wait(sem, 3 + LINE * PAIR - 1)

    def lo_out(kind, i, src, dst):
        res = []
        for j, (yy, cc) in enumerate(peers):
            mm_ = yy * 2 + cc
            res.append(rcopy(src.at[S.imgs * mm_ + i], dst.at[m, i], lo_send.at[kind, j, i], lo_recv.at[kind, m, i], dev(yy, cc)))
        return res

    def lo_in(kind, i, dst):
        return [rcopy(dst.at[yy * 2 + cc, i], dst.at[yy * 2 + cc, i], lo_send.at[kind, j, i], lo_recv.at[kind, yy * 2 + cc, i], dev(yy, cc)) for j, (yy, cc) in enumerate(peers)]

    def lo_local(kind, i, src, dst):
        return pltpu.make_async_copy(src.at[S.imgs * m + i], dst.at[m, i], local.at[kind, i])

    def lo_back(kind, i, src, dst):
        return [rcopy(src.at[yy * 2 + cc, i], dst.at[S.imgs * m + i], lo_send.at[kind, j, i], lo_recv.at[kind, m, i], dev(yy, cc)) for j, (yy, cc) in enumerate(peers)]

    def lo_back_in(kind, i, dst):
        return [rcopy(dst.at[S.imgs * (yy * 2 + cc) + i], dst.at[S.imgs * (yy * 2 + cc) + i], lo_send.at[kind, j, i], lo_recv.at[kind, yy * 2 + cc, i], dev(yy, cc)) for j, (yy, cc) in enumerate(peers)]

    def lo_back_local(kind, i, src, dst):
        return pltpu.make_async_copy(src.at[m, i], dst.at[S.imgs * m + i], local.at[kind, i])

    def hi_out(kind, src, dst):
        res = []
        for h in range(2):
            mine = (y == h) & (c == y)
            ref = src.at[h] if src.shape[0] == 2 and len(src.shape) == 3 else src
            res.append((mine, rcopy(ref, dst.at[c], hi_send.at[kind, h], hi_recv.at[kind, c], dev(h, y)),
                        pltpu.make_async_copy(ref, dst.at[c], local.at[kind, S.imgs])))
        return res

    def hi_in(kind, dst):
        res = []
        for j in range(2):
            mine = (y == c) & (c == j)
            res.append((mine, rcopy(dst.at[j], dst.at[j], hi_send.at[kind, j], hi_recv.at[kind, j], dev(c, j))))
        return res

    def hi_back(kind, src, dst):
        res = []
        for j in range(2):
            mine = (y == c) & (c == j)
            res.append((mine, rcopy(src.at[j], dst.at[y], hi_send.at[kind, j], hi_recv.at[kind, y], dev(c, j)),
                        pltpu.make_async_copy(src.at[j], dst.at[y], local.at[kind, S.imgs])))
        return res

    def hi_back_in(kind, dst):
        res = []
        for h in range(2):
            mine = (y == h) & (c == y)
            res.append((mine, rcopy(dst.at[h], dst.at[h], hi_send.at[kind, h], hi_recv.at[kind, h], dev(h, y))))
        return res

    def start(copies):
        for cp in copies:
            cp.start()

    def start_hi(copies):
        for mine, remote, here in copies:
            pl.when(mine)(here.start)
            pl.when(jnp.logical_not(mine))(remote.start)

    def sent_hi(copies):
        for mine, remote, here in copies:
            pl.when(mine)(here.wait)
            pl.when(jnp.logical_not(mine))(remote.wait_send)

    def got_hi(copies):
        for mine, remote in copies:
            pl.when(jnp.logical_not(mine))(remote.wait_recv)

    my = (1 - y) * 2 + c

    def across(v, lanes):
        n = v.shape[0]
        return jnp.broadcast_to(v[...].astype(f32).reshape(1, n), (lanes, n)).T.astype(bf16)

    start_hi(hi_out(0, x_hi, xh))
    wg[m] = jnp.zeros((S.blocks, S.ks, 256), bf16)
    wg[m, 0, :, 128:256] = across(b1l, 128)
    wg[m, 1 + S.hb, :, 128:256] = across(b1h, 128)
    wg[m, 0, :, 0:S.pr] = jnp.zeros((S.ks, S.pr), bf16)
    wg[m, 0, :, 0:S.p] = w1l[...]
    wg[m, 1, :, 0:S.p] = w2l[...]
    for j in range(S.hb):
        n = min(256, S.ph - 256 * j)
        wg[m, 2 + j, :, 0:n] = w1h[:, 256 * j:256 * j + n]
        wg[m, 2 + S.hb + j, :, 0:n] = w2h[:, 256 * j:256 * j + n]
    w_y = rcopy(wg.at[m, dpi], wg.at[m, dpi], w_send.at[0], w_recv.at[0], dev(1 - y, c))
    w_y_in = rcopy(wg.at[my, dpi], wg.at[my, dpi], w_send.at[0], w_recv.at[0], dev(1 - y, c))
    w_c = rcopy(wg.at[m], wg.at[m], w_send.at[1], w_recv.at[1], dev(y, 1 - c))
    w_f = rcopy(wg.at[my], wg.at[my], w_send.at[2], w_recv.at[2], dev(y, 1 - c))
    w_d = [rcopy(wg.at[my, dpi], wg.at[my, dpi], w_send.at[6 + k], w_recv.at[7 + dpi], dp_dev(k)) for k in range(1, LINE * PAIR)]
    w_y.start()
    w_c.start()
    bl[m] = across(b2l, 128)
    bias_out = [rcopy(bl.at[m], bl.at[m], w_send.at[3 + j], w_recv.at[3 + m], dev(yy, cc)) for j, (yy, cc) in enumerate(peers)]
    start(bias_out)
    bho[...] = across(b2h, 128)
    bias_hi_out = hi_out(4, bho, bh)
    start_hi(bias_hi_out)
    for i in range(S.imgs):
        start(lo_out(0, i, x_lo, xl))
        lo_local(0, i, x_lo, xl).start()
    start_hi(hi_out(1, cot_hi, ch))
    for i in range(S.imgs):
        start(lo_out(1, i, cot_lo, cl))
        lo_local(1, i, cot_lo, cl).start()
    load_in = pltpu.make_async_copy(w_in, winv, local.at[4, 1])
    load_out = pltpu.make_async_copy(w_out, woutv, local.at[4, 2])
    load_in.start()
    load_out.start()

    def line_of(v):
        return v[...].astype(f32).reshape(1, v.shape[0])

    gv1, sv1 = line_of(gain1), line_of(shift1)
    gv2, sv2 = line_of(gain2), line_of(shift2)
    brow[...] = line_of(b_in)
    hi = pl.ds(S.hi0, S.own)
    own = pl.ds(pl.multiple_of(c * S.own, 16), S.own)

    def img(i):
        return pl.ds(pl.multiple_of(i * S.pr, 16), S.pr)

    def gather_rows(block, i):
        for s in range(4):
            tmp[s * S.q:(s + 1) * S.q, :] = block[s, i].astype(f32)
        if S.pr > S.p:
            tmp[S.p:S.pr, :] = jnp.zeros((S.pr - S.p, d), f32)

    def scatter_rows(block, i):
        for s in range(4):
            block[s, i] = tmp[s * S.q:(s + 1) * S.q, :].astype(bf16)

    sv[...] = jnp.zeros_like(sv)
    t[...] = jnp.zeros_like(t)
    gw1[...] = jnp.zeros_like(gw1)
    gw2[...] = jnp.zeros_like(gw2)

    got_hi(hi_in(0, xh))
    sent_hi(hi_out(0, x_hi, xh))
    v = xh[...].reshape(S.own, d).astype(f32)
    cen, rs = centred(v)
    n = (cen * rs * gv1 + sv1).astype(bf16)
    nb[hi, :] = n
    nh[own, :] = n
    af[hi, :] = v
    nh_copy = rcopy(nh.at[own], nh.at[own], ring_send.at[0], ring_recv.at[0], dev(y, 1 - c))
    nh_copy.start()

    w_y.wait_send()
    w_y_in.wait_recv()
    start(w_d)
    for k in range(1, LINE * PAIR):
        i = (dpi + k) % (LINE * PAIR)
        w_d[k - 1].wait_send()
        rcopy(wg.at[my, i], wg.at[my, i], w_send.at[6 + k], w_recv.at[7 + i], dp_dev(k)).wait_recv()
    w_f.start()
    w_c.wait()
    w_f.wait_send()
    w_far = rcopy(wg.at[(1 - y) * 2 + 1 - c], wg.at[(1 - y) * 2 + 1 - c], w_send.at[2], w_recv.at[2], dev(y, 1 - c))
    w_far.wait_recv()

    def block(b, n):
        return wg[:, b, :, 0:n].reshape(S.k, n)

    def w1t_lo():
        return block(0, S.pr)

    def w2_lo():
        return block(1, S.pr)

    def bias_of(b):
        return wg[:, b, :, 128:256].reshape(S.k, 128).astype(f32)[:, 127:128]

    spans = [(256 * j, min(256, S.ph - 256 * j)) for j in range(S.hb)]

    def mm_hi(first, rows_of):
        return functools.reduce(jnp.add, [mm(block(first + j, n), rows_of[at:at + n, :]) for j, (at, n) in enumerate(spans)])

    for k in range(2):
        bcols[k] = jnp.broadcast_to(bias_of(k * (1 + S.hb)), (S.k, 128))

    def b1_lo():
        return bcols[0, :, 0:1]

    def b1_hi():
        return bcols[1, :, 0:1]

    w1_lo[...] = w1t_lo().T
    w2t_lo[...] = w2_lo().T
    for j, (at, n) in enumerate(spans):
        w1_hi[at:at + n, :] = block(2 + j, n).T
        w2t_hi[at:at + n, :] = block(2 + S.hb + j, n).T
    for j, (yy, cc) in enumerate(peers):
        bias_out[j].wait_send()
        s = yy * 2 + cc
        rcopy(bl.at[s], bl.at[s], w_send.at[3 + j], w_recv.at[3 + s], dev(yy, cc)).wait_recv()
    got_hi(hi_in(4, bh))
    sent_hi(bias_hi_out)
    bcol[...] = jnp.zeros_like(bcol)
    for s in range(4):
        bcol[s * S.q:(s + 1) * S.q, :] = bl[s].astype(f32)

    def fwd_lo(i, carry):
        for cp in lo_in(0, i, xl):
            cp.wait_recv()
        lo_local(0, i, x_lo, xl).wait()
        gather_rows(xl, i)
        v = tmp[...]
        cen, rs = centred(v)
        n = (cen * rs * gv1 + sv1).astype(bf16)
        nb[img(i), :] = n
        ht = gelu(mm(w1t_lo(), n) + b1_lo()).astype(bf16)
        af[img(i), :] = v + (mm(w2t_lo[...], ht) + bcol[:, 0:1])
        return carry

    lax.fori_loop(0, S.imgs, fwd_lo, 0)
    nh_copy.wait()
    ht = gelu(mm_hi(2, nh) + b1_hi()).astype(bf16)
    bcol_hi = bh[...].reshape(S.own, 128).astype(f32)[:, 0:1]
    af[hi, :] = af[hi, :] + (mm(w2t_hi[own, :], ht) + bcol_hi)

    def norm_two(rows):
        cen, rs = centred(af[rows, :])
        n2[rows, :] = (cen * rs * gv2 + sv2).astype(bf16)

    norm_two(hi)

    def norm_lo(i, carry):
        norm_two(img(i))
        return carry

    lax.fori_loop(0, S.imgs, norm_lo, 0)

    def live_lo(i):
        return jnp.where(S.imgs * m + i < counts[0, 0], 1.0, 0.0).astype(f32)

    live_hi = jnp.where(y < counts[0, 1], 1.0, 0.0).astype(f32)
    got_hi(hi_in(1, ch))
    sent_hi(hi_out(1, cot_hi, ch))
    ct[hi, :] = (ch[...].reshape(S.own, d).astype(f32) * live_hi).astype(bf16)

    def cot_rows(i, carry):
        for cp in lo_in(1, i, cl):
            cp.wait_recv()
        lo_local(1, i, cot_lo, cl).wait()
        gather_rows(cl, i)
        ct[img(i), :] = (tmp[...] * live_lo(i)).astype(bf16)
        return carry

    lax.fori_loop(0, S.imgs, cot_rows, 0)
    for kind, src, dst in ((0, x_lo, xl), (1, cot_lo, cl)):
        for i in range(S.imgs):
            for cp in lo_out(kind, i, src, dst):
                cp.wait_send()
    load_in.wait()
    load_out.wait()

    def channel(f):
        cols = pl.ds(pl.multiple_of(f * CHUNK, CHUNK), CHUNK)
        h, slope = gelu_both(mm(n2[...], winv[:, cols]) + brow[:, cols])
        hb = h.astype(bf16)
        hid[:, cols] = hb
        gpre = (mm(ct[...], woutv[cols, :], 1, 1) * slope).astype(bf16)
        gp[:, cols] = gpre
        gb[:, cols] = colsum(gpre.astype(f32))
        g[f, 0:d, :] = mm(n2[...], gpre, 0, 0).astype(bf16)
        grad = mm(hb, ct[...], 0, 0)
        for j in range(d // 256):
            g[f, S.half_rows + CHUNK * j:S.half_rows + CHUNK * (j + 1), :] = grad[:, 256 * j:256 * (j + 1)].astype(bf16)

    bo = line_of(b_out)

    def channel_back(rows, live):
        a = af[rows, :]
        out = (a + mm(hid[rows, :], woutv[...]) + bo) * live
        gn = mm(gp[rows, :], winv[...], 1, 1)
        cen, rs = centred(a)
        c_rows = ct[rows, :].astype(f32)
        grad = c_rows + norm_back(cen, rs, gn * gv2)
        sv[0:1, :] += colsum(c_rows)
        sv[1:2, :] += colsum(gn * (cen * rs))
        sv[2:3, :] += colsum(gn)
        af[rows, :] = grad
        n2[rows, :] = grad.astype(bf16)
        return out

    def back_hi():
        out = channel_back(hi, live_hi)
        ch[...] = out.astype(bf16).reshape(2, S.qh, d)
        gmh[own, :] = n2[hi, :]
        gm_copy.start()

    gm_copy = rcopy(gmh.at[own], gmh.at[own], ring_send.at[1], ring_recv.at[1], dev(y, 1 - c))

    def back_lo(i):
        tmp[...] = channel_back(img(i), live_lo(i))
        scatter_rows(cl, i)

    ones = jnp.ones((8, d), bf16)

    def first_norm_back(v, gn, rows):
        cen, rs = centred(v)
        sv[3:4, :] += colsum(gn * (cen * rs))
        sv[4:5, :] += colsum(gn)
        return af[rows, :] + norm_back(cen, rs, gn * gv1)

    def token_lo(i):
        n = nb[img(i), :]
        gm = n2[img(i), :]
        h, slope = gelu_both(mm(w1t_lo(), n) + b1_lo())
        gw2[:, 0:S.pr] += mm(h.astype(bf16), gm, 1, 1)
        gpt = (mm(w2_lo(), gm) * slope).astype(bf16)
        gw1[:, 0:S.pr] += mm(gpt, n, 1, 1)
        sv[9:10, 0:S.k] += mm(ones, gpt, 1, 1)[0:1]
        sv[10:11, 0:S.pr] += mm(ones, gm, 1, 1)[0:1]
        gn = mm(w1_lo[...], gpt)
        gather_rows(xl, i)
        tmp[...] = first_norm_back(tmp[...], gn, img(i))
        scatter_rows(xl, i)
        start(lo_back(3, i, xl, grad_lo))
        lo_back_local(3, i, xl, grad_lo).start()

    def token_hi():
        gm_copy.wait()
        n = nb[hi, :]
        gm = n2[hi, :]
        h, slope = gelu_both(mm_hi(2, nh) + b1_hi())
        ga2 = mm(h.astype(bf16), gmh[...], 1, 1) * 0.5
        gpt = (mm_hi(2 + S.hb, gmh) * slope).astype(bf16)
        ga1 = mm(gpt, nh[...], 1, 1) * 0.5
        sv[11:12, 0:S.k] += mm(ones, gpt, 1, 1)[0:1] * 0.5
        sv[pl.ds(12 + c, 1), 0:S.own] = mm(ones, gm, 1, 1)[0:1]
        gn = mm(w1_hi[own, :], gpt)
        grad = first_norm_back(xh[...].reshape(S.own, d).astype(f32), gn, hi)
        xh[...] = grad.astype(bf16).reshape(2, S.qh, d)
        start_hi(hi_back(3, xh, grad_hi))
        for j in range(S.ff // d):
            sv[5 + j:6 + j, :] = gb[:, d * j:d * (j + 1)]
        s1[m] = sv[...]
        start(s1_out)
        for ks in range(4):
            k0, yy, cc = ks * S.ks, ks // 2, ks % 2

            def put(j, v, n=256):
                row = (cc * SHARDS + 2 * j + yy) * S.ks
                t[0, row:row + S.ks, 0:n] = v.astype(bf16)

            put(0, gw1[k0:k0 + S.ks, :])
            put(1, gw2[k0:k0 + S.ks, :])
            for j in range(S.hb):
                n = min(256, S.ph - 256 * j)
                put(2 + j, ga1[k0:k0 + S.ks, 256 * j:256 * j + n], n)
                put(2 + S.hb + j, ga2[k0:k0 + S.ks, 256 * j:256 * j + n], n)

    s1_out = [rcopy(s1.at[m], s1.at[m], s_send.at[j], s_recv.at[m], dev(yy, cc)) for j, (yy, cc) in enumerate(peers)]
    s2_out = [rcopy(s2.at[dpi], s2.at[dpi], s_send.at[3 + k], s_recv.at[4 + dpi], dp_dev(k)) for k in range(1, LINE * PAIR)]

    ar = AllReduce(p, g, g_core, g_land, g_sum, g_send, g_recv, g_kept)
    art = TokenSum(p, t, t_core, t_land, t_sum, t_send, t_recv, t_kept)
    nc = S.chunks
    b0 = nc + 1 + S.imgs
    t0 = b0 + S.imgs

    def send_out(k):
        start(lo_back(2, k, cl, out_lo))
        lo_back_local(2, k, cl, out_lo).start()

    def step(i, carry):
        pl.when(i < nc)(lambda: channel(i))
        pl.when(i == nc)(back_hi)
        pl.when((i > nc) & (i < b0))(lambda: back_lo(i - nc - 1))
        pl.when((i >= b0) & (i < t0))(lambda: token_lo(i - b0))
        pl.when(i == t0)(token_hi)
        pl.when(i == t0 + 2)(small_sums)
        pl.when(i == t0 + 2)(lambda: start_hi(hi_back(2, ch, out_hi)))
        for k in range(S.imgs):
            pl.when(i == t0 + 4 + 2 * k)(functools.partial(send_out, k))
        ar.step(i, nc, paths, OFFSETS)
        art.step(i - t0, T_OFFSETS)
        return carry

    def small_sums():
        for j, (yy, cc) in enumerate(peers):
            s = yy * 2 + cc
            s1_out[j].wait_send()
            rcopy(s1.at[s], s1.at[s], s_send.at[j], s_recv.at[s], dev(yy, cc)).wait_recv()
        s2[dpi] = s1[0] + s1[1] + s1[2] + s1[3]
        start(s2_out)

    lax.fori_loop(0, max(nc + OFFSETS[-1], t0 + 1 + T_OFFSETS[-1]), step, 0)
    for k in range(1, LINE * PAIR):
        i = (dpi + k) % (LINE * PAIR)
        s2_out[k - 1].wait_send()
        rcopy(s2.at[i], s2.at[i], s_send.at[3 + k], s_recv.at[4 + i], dp_dev(k)).wait_recv()
    total = s2[0]
    for i in range(1, LINE * PAIR):
        total = total + s2[i]
    s_sum[...] = total

    for kind, src, src_hi, dst, dst_hi in ((2, cl, ch, out_lo, out_hi), (3, xl, xh, grad_lo, grad_hi)):
        for i in range(S.imgs):
            for cp in lo_back(kind, i, src, dst):
                cp.wait_send()
            for cp in lo_back_in(kind, i, dst):
                cp.wait_recv()
            lo_back_local(kind, i, src, dst).wait()
        sent_hi(hi_back(kind, src_hi, dst_hi))
        got_hi(hi_back_in(kind, dst_hi))


def mixer(S, args):
    V = pl.BlockSpec(memory_space=pltpu.VMEM)
    A = pl.BlockSpec(memory_space=pl.ANY)
    M = pl.BlockSpec(memory_space=pltpu.SMEM)
    sds = jax.ShapeDtypeStruct
    d, dma = S.d, pltpu.SemaphoreType.DMA
    nc = S.chunks
    unit = 2 * S.half_rows // (2 * SHARDS)
    scratch = [
        pltpu.VMEM((4, S.imgs, S.q, d), bf16), pltpu.VMEM((2, S.qh, d), bf16),
        pltpu.VMEM((4, S.imgs, S.q, d), bf16), pltpu.VMEM((2, S.qh, d), bf16),
        pltpu.VMEM((4, S.blocks, S.ks, 256), bf16), pltpu.VMEM((4, S.q, 128), bf16), pltpu.VMEM((S.qh, 128), bf16), pltpu.VMEM((2, S.qh, 128), bf16),
        pltpu.VMEM((S.pr, S.k), bf16), pltpu.VMEM((S.pr, S.k), bf16), pltpu.VMEM((S.ph, S.k), bf16), pltpu.VMEM((S.ph, S.k), bf16),
        pltpu.VMEM((S.pr, 128), f32), pltpu.VMEM((2, S.k, 128), f32), pltpu.VMEM((1, S.ff), f32),
        pltpu.VMEM((S.rows, d), f32), pltpu.VMEM((S.rows, d), bf16), pltpu.VMEM((S.ph, d), bf16), pltpu.VMEM((S.rows, d), bf16),
        pltpu.VMEM((S.rows, d), bf16), pltpu.VMEM((S.pr, d), f32), pltpu.VMEM((S.ph, d), bf16),
        pltpu.VMEM((S.rows, S.ff), bf16), pltpu.VMEM((S.rows, S.ff), bf16), pltpu.VMEM((d, S.ff), bf16), pltpu.VMEM((S.ff, d), bf16),
        pltpu.VMEM((nc, 2 * SHARDS * unit, 256), bf16), pltpu.VMEM((CORE_SLOTS, SHARDS * unit, 256), bf16), pltpu.VMEM((nc, LANDED * unit, 256), bf16),
        pltpu.VMEM((1, 2 * SHARDS * S.ks, 256), bf16), pltpu.VMEM((1, SHARDS * S.ks, 256), bf16), pltpu.VMEM((1, LANDED * S.ks, 256), bf16),
        pltpu.VMEM((S.k, 256), f32), pltpu.VMEM((S.k, 256), f32), pltpu.VMEM((1, S.ff), f32),
        pltpu.VMEM((SMALL, d), f32), pltpu.VMEM((4, SMALL, d), f32), pltpu.VMEM((LINE * PAIR, SMALL, d), f32),
        dma((4, 3, S.imgs)), dma((4, 4, S.imgs)), dma((5, 2)), dma((5, 2)), dma((14,)), dma((15,)), dma((2,)), dma((2,)),
        dma((nc, NSEM)), dma((nc, NSEM)), dma((1, NSEM)), dma((1, NSEM)), dma((11,)), dma((12,)), dma((5, S.imgs + 1)), dma((nc,)), dma((1,)),
    ]
    return pl.pallas_call(
        functools.partial(kernel, S),
        out_shape=(
            sds((S.slots, S.q, d), bf16), sds((2, S.qh, d), bf16), sds((S.slots, S.q, d), bf16), sds((2, S.qh, d), bf16),
            sds((nc, 2 * S.half_rows, 256), bf16), sds((1, S.blocks * S.ks, 256), bf16), sds((SMALL, d), f32),
        ),
        in_specs=[A, A, A, A, M] + [V] * 8 + [A, A] + [V] * 6,
        out_specs=(A, A, A, A, A, A, V),
        scratch_shapes=scratch,
        compiler_params=pltpu.CompilerParams(collective_id=0, has_side_effects=True, vmem_limit_bytes=63 * 1024 * 1024),
    )(*args)


class TokenSum(AllReduce):
    def part(self, i):
        return self.out.at[0, self.sh(i, 1)]

    def line_back(self, f, path, k):
        z, base = self.p.z, self.p.x * LINE
        inside = lambda p: self.part(base + jnp.clip(p, 0, LINE - 1))
        up, down = inside(z + 1 - k), inside(z + k - 1)
        up_src, down_src, more = up, down, []
        if k == 1:
            up_src = down_src = self.half(f, (base + z) * PAIR + self.p.y, 1)
            more = [(None, None, pltpu.make_async_copy(up_src, up, self.kept.at[f]), None)]
        return [((z < LINE - 1) & (z >= k - 1), (z > 0) & (z >= k), self.copy(f, UP_BACK + k, up_src, up, self.p.up()), None),
                ((z > 0) & (z <= LINE - k), (z < LINE - 1) & (z <= LINE - 1 - k), self.copy(f, DOWN_BACK + k, down_src, down, self.p.down()), None)] + more

    def x_back(self, f):
        ref = self.out.at[0, self.sh(self.p.x * LINE, LINE)]
        return [(None, None, self.copy(f, X_BACK, ref, ref, self.p.pair("x")), None)]

    def steps(self, path):
        there = super().steps(path)[:2 + LINE]
        return there + [functools.partial(self.line_back, path=path, k=k) for k in range(1, LINE)] + [self.x_back]

    def step(self, i, offsets):
        for s in range(len(offsets)):
            pl.when(i == offsets[s])(functools.partial(self.run_stage, 0, s, "xzy"))


def finish(S, out_lo, out_hi, grad_lo, grad_hi, g, t, s):
    d = S.d
    sds = jax.ShapeDtypeStruct
    per = 2

    def place(ol, oh, gl, gh, g_ref, t_ref, s_ref, *outs):
        (o_lo, o_hi, r_lo, r_hi, l1g, l1b, w1l, b1l, w2l, b2l, w1h, b1h, w2h, b2h, l2g, l2b, w_in, b_in, w_out, b_out) = outs
        m = lax.axis_index("mp")
        for k in range(per):
            at = slice(CHUNK * k, CHUNK * (k + 1))
            w_in[:, at] = g_ref[k, 0:d, :].astype(f32)
            for j in range(d // 256):
                w_out[at, 256 * j:256 * (j + 1)] = g_ref[k, S.half_rows + CHUNK * j:S.half_rows + CHUNK * (j + 1), :].astype(f32)
        o_lo[...] = ol[...]
        r_lo[...] = gl[...].astype(f32)

        @pl.when(pl.program_id(0) == 0)
        def _():
            o_hi[...] = oh[...]
            r_hi[...] = gh[...].astype(f32)
            w1l[...] = t_ref[0, :, 0:S.p].astype(f32)
            w2l[...] = t_ref[1, :, 0:S.p].astype(f32)
            for j in range(S.hb):
                n = min(256, S.ph - 256 * j)
                w1h[:, 256 * j:256 * j + n] = t_ref[2 + j, :, 0:n].astype(f32)
                w2h[:, 256 * j:256 * j + n] = t_ref[2 + S.hb + j, :, 0:n].astype(f32)
            for i, o in ((0, b_out), (1, l2g), (2, l2b), (3, l1g), (4, l1b)):
                o[...] = s_ref[i, :]
            for j in range(S.ff // d):
                b_in[d * j:d * (j + 1)] = s_ref[5 + j, :]
            for j in range(4):
                @pl.when(m == j)
                def _():
                    b1l[...] = s_ref[9, S.ks * j:S.ks * (j + 1)]
                    b2l[...] = s_ref[10, S.q * j:S.q * (j + 1)]
                    b1h[...] = s_ref[11, S.ks * j:S.ks * (j + 1)]
                    b2h[...] = s_ref[12 + j // 2, S.qh * (j % 2):S.qh * (j % 2 + 1)]

    def whole(v):
        return pl.BlockSpec(v.shape, lambda i: (0,) * len(v.shape))

    image = pl.BlockSpec((per * S.slots // S.chunks, S.q, d), lambda i: (i, 0, 0))
    vec = lambda n: sds((n,), f32)
    shapes = [
        sds(out_lo.shape, bf16), sds(out_hi.shape, bf16), sds(out_lo.shape, f32), sds(out_hi.shape, f32), vec(d), vec(d),
        sds((S.ks, S.p), f32), vec(S.ks), sds((S.ks, S.p), f32), vec(S.q), sds((S.ks, S.ph), f32), vec(S.ks), sds((S.ks, S.ph), f32), vec(S.qh),
        vec(d), vec(d), sds((d, S.ff), f32), vec(S.ff), sds((S.ff, d), f32), vec(d),
    ]
    outs = [whole(v) for v in shapes]
    outs[0] = outs[2] = image
    outs[16] = pl.BlockSpec((d, per * CHUNK), lambda i: (0, i))
    outs[18] = pl.BlockSpec((per * CHUNK, d), lambda i: (i, 0))
    t = t.reshape(S.blocks, S.ks, 256)
    return pl.pallas_call(
        place,
        grid=(S.chunks // per,),
        out_shape=shapes,
        in_specs=[image, whole(out_hi), image, whole(grad_hi), pl.BlockSpec((per, 2 * S.half_rows, 256), lambda i: (i, 0, 0)), whole(t), whole(s)],
        out_specs=outs,
        compiler_params=pltpu.CompilerParams(vmem_limit_bytes=63 * 1024 * 1024),
    )(out_lo, out_hi, grad_lo, grad_hi, g, t, s)


def body(
    groups,
    x_lo, x_hi, cot_lo, cot_hi, counts, ln1_gain, ln1_bias, w_tok1_lo, b_tok1_lo, w_tok2_lo, b_tok2_lo, w_tok1_hi, b_tok1_hi,
    w_tok2_hi, b_tok2_hi, ln2_gain, ln2_bias, w_chan_in, b_chan_in, w_chan_out, b_chan_out,
):
    w1_lo, w1_hi = w_tok1_lo.T, w_tok1_hi.T
    S = Sizes(x_lo, x_hi, w1_lo, w_chan_in)
    out_lo, out_hi, grad_lo, grad_hi, g, t, s = mixer(
        S,
        (x_lo, x_hi, cot_lo, cot_hi, counts, w1_lo, b_tok1_lo, w_tok2_lo, b_tok2_lo, w1_hi, b_tok1_hi, w_tok2_hi, b_tok2_hi,
         w_chan_in, w_chan_out, b_chan_in, b_chan_out, ln1_gain, ln1_bias, ln2_gain, ln2_bias),
    )
    if groups is not None:
        g, t, s = lax.psum((g.astype(f32), t.astype(f32), s), "dp", axis_index_groups=groups)
    res = list(finish(S, out_lo, out_hi, grad_lo, grad_hi, g, t, s))
    res[6], res[10] = res[6].T, res[10].T
    return tuple(res)


def solution(mesh):
    blocks = mesh.shape["dp"] // (LINE * PAIR)
    groups = None
    if blocks > 1:
        size = LINE * PAIR
        groups = [[b * size + i for b in range(blocks)] for i in range(size)]
    tokens, rows = P("dp", "mp", None), P("dp", None)
    col, row, vec, rep = P(None, "mp"), P("mp", None), P("mp"), P()
    return jax.shard_map(
        functools.partial(body, groups),
        mesh=mesh,
        in_specs=(tokens,) * 4 + (rows, rep, rep) + (col, vec, row, vec) * 2 + (rep,) * 6,
        out_specs=(tokens,) * 4 + (rep, rep) + (col, vec, row, vec) * 2 + (rep,) * 6,
        check_vma=False,
    )
```
